32 devices in a mesh: dp: 4 (over z), fsdp: 8 (over y, x, core).
Axes of the slice: x: 2, y: 2, z: 4, core: 2. Of those that a mesh axis runs over, the one named last changes fastest.
Arguments:
- tokens: bfloat16 [32768, 768], P(('dp', 'fsdp')), may hold values from -6 to 6
- cotangent: bfloat16 [32768, 768], P(('dp', 'fsdp')), may hold values from -6 to 6
- crop_rows: int32 [128], P(('dp', 'fsdp')), may hold values from 12 to 16, as said below
- crop_top: int32 [128], P(('dp', 'fsdp')), may hold values from 0 to 4, as said below
- attn_gain: bfloat16 [768], P('fsdp'), may hold values from 0.5 to 1.5
- attn_shift: bfloat16 [768], P('fsdp'), may hold values from -1.5 to 1.5
- heads_weight: bfloat16 [768, 2304], P('fsdp'), may hold values from -0.3125 to 0.3125
- heads_bias: bfloat16 [1536], P('fsdp'), may hold values from -2.5 to 2.5
- proj_weight: bfloat16 [768, 768], P('fsdp'), may hold values from -0.625 to 0.625
- proj_bias: bfloat16 [768], P('fsdp'), may hold values from -2.5 to 2.5
- mlp_gain: bfloat16 [768], P('fsdp'), may hold values from 0.5 to 1.5
- mlp_shift: bfloat16 [768], P('fsdp'), may hold values from -1.5 to 1.5
- up_weight: bfloat16 [768, 3072], P('fsdp'), may hold values from -0.21875 to 0.21875
- up_bias: bfloat16 [3072], P('fsdp'), may hold values from -2.5 to 2.5
- down_weight: bfloat16 [3072, 768], P('fsdp'), may hold values from -0.15625 to 0.15625
- down_bias: bfloat16 [768], P('fsdp'), may hold values from -2.5 to 2.5
Outputs:
- block_out: bfloat16 [32768, 768], P(('dp', 'fsdp'))
- tokens_grad: bfloat16 [32768, 768], P(('dp', 'fsdp'))
- attn_gain_grad: float32 [768], P('fsdp')
- attn_shift_grad: float32 [768], P('fsdp')
- heads_weight_grad: float32 [768, 2304], P('fsdp')
- heads_bias_grad: float32 [1536], P('fsdp')
- proj_weight_grad: float32 [768, 768], P('fsdp')
- proj_bias_grad: float32 [768], P('fsdp')
- mlp_gain_grad: float32 [768], P('fsdp')
- mlp_shift_grad: float32 [768], P('fsdp')
- up_weight_grad: float32 [768, 3072], P('fsdp')
- up_bias_grad: float32 [3072], P('fsdp')
- down_weight_grad: float32 [3072, 768], P('fsdp')
- down_bias_grad: float32 [768], P('fsdp')
The draws below stay inside these ranges and needn't reach their ends.
Inputs may be any that keep to these rules, and one draw needn't show every extreme that they name: Image b's crop holds crop_rows[b] whole grid rows of 16 slots each. Image b's crop fills grid rows crop_top[b] to crop_top[b] + crop_rows[b] - 1, all within the 16 rows.
All inputs are finite; a program needn't handle non-finite values.
Results may differ from the reference program's by a relative error of at most 0.019.
Values may be sent and summed in bfloat16 or wider, within the bound.
A program may use at most 192 MiB of HBM per device.

```python
import math
import jax
import jax.numpy as jnp
from jax import lax

D = 768
HEADS = 16
HEAD = 48
FF = 3072
GRID = 16
SLOTS = 256
IMAGES = 128
TOKENS = 32768


def crop_choice(key):
    heights = jax.random.randint(key, (IMAGES,), GRID - GRID // 4, GRID + 1, dtype=jnp.int32)
    tall_one = jax.random.randint(jax.random.fold_in(key, 11), (), 0, IMAGES, dtype=jnp.int32)
    offset = jax.random.randint(jax.random.fold_in(key, 12), (), 1, IMAGES, dtype=jnp.int32)
    short_one = (tall_one + offset) % IMAGES
    places = jnp.arange(IMAGES, dtype=jnp.int32)
    heights = jnp.where(places == tall_one, GRID, heights)
    heights = jnp.where(places == short_one, GRID - GRID // 4, heights)
    return (heights.astype(jnp.int32), places == short_one)


def draw_crop_rows(key, part):
    heights, marked = crop_choice(key)
    return heights


def draw_crop_top(key, part):
    heights, marked = crop_choice(key)
    key = jax.random.fold_in(key, 5)
    spare = GRID - heights
    starts = jax.random.randint(key, (IMAGES,), 0, spare + 1, dtype=jnp.int32)
    return jnp.where(marked, spare, starts).astype(jnp.int32)


def strengthened(values, key, source, target, parts, factor):
    owner, partner = [(jnp.arange(values.shape[position]) // (values.shape[position] // parts)).reshape([-1 if axis == position else 1 for axis in range(values.ndim)]) for position in (source, target)]
    chosen = jax.random.permutation(key, parts)[partner]
    strong = (owner == chosen) | (owner == (partner + parts // 2) % parts)
    return jnp.where(strong, factor * values, values)


def block_scale(rng, dims, cuts, least, largest):
    def one(axis_at, parts):
        draws = jax.random.uniform(jax.random.fold_in(jax.random.fold_in(rng, 6), axis_at), (parts,), jnp.float32, least / len(cuts), largest / len(cuts))
        return jnp.repeat(jnp.exp(draws), dims[axis_at] // parts).reshape((-1,) + (1,) * (len(dims) - axis_at - 1))

    loudness = one(*cuts[0])
    for cut in cuts[1:]:
        loudness = loudness * one(*cut)
    return loudness


def centred(stream_key, dims, deviation, limit, cuts=(), kind=jnp.bfloat16):
    drawn = deviation * jax.random.normal(stream_key, dims, jnp.float32)
    if cuts:
        drawn = drawn * block_scale(stream_key, dims, cuts, -0.22, 0.18)
    return jnp.clip(drawn, -limit, limit).astype(kind)


def gaussian_with(rng, extent, width, most, cuts, heavy, held_as=jnp.bfloat16):
    array = width * jax.random.normal(rng, extent, jnp.float32)
    if cuts:
        array = array * block_scale(rng, extent, cuts, -0.22, 0.18)
    return jnp.clip(strengthened(array, jax.random.fold_in(rng, 3), *heavy), -most, most).astype(held_as)


def setup_inputs(seed: int = 0) -> dict:
    key_of = jax.random.split(jax.random.key(seed), 17)
    return {
        "tokens": centred(key_of[0], (TOKENS, D), 1.0, 6.0, ((0, 32),)),
        "cotangent": gaussian_with(key_of[1], (TOKENS, D), 1.0, 6.0, ((0, 32),), (0, 1, 32, 2.75)),
        "crop_rows": draw_crop_rows(jax.random.fold_in(key_of[16], 71), 0),
        "crop_top": draw_crop_top(jax.random.fold_in(key_of[16], 71), 0),
        "attn_gain": jnp.clip(1.0 + 0.1 * jax.random.normal(key_of[4], (D,), jnp.float32), 0.5, 1.5).astype(jnp.bfloat16),
        "attn_shift": centred(key_of[5], (D,), 0.3, 1.5, ((0, 8),)),
        "heads_weight": centred(key_of[6], (D, 3 * D), (D // 2) ** -0.5, 0.3125, ((0, 8),)),
        "heads_bias": centred(key_of[7], (2 * D,), 0.5, 2.5, ((0, 8),)),
        "proj_weight": centred(key_of[8], (D, D), (D // 8) ** -0.5, 0.625, ((0, 8),)),
        "proj_bias": centred(key_of[9], (D,), 0.5, 2.5, ((0, 8),)),
        "mlp_gain": jnp.clip(1.0 + 0.1 * jax.random.normal(key_of[10], (D,), jnp.float32), 0.5, 1.5).astype(jnp.bfloat16),
        "mlp_shift": centred(key_of[11], (D,), 0.3, 1.5, ((0, 8),)),
        "up_weight": centred(key_of[12], (D, FF), D ** -0.5, 0.21875, ((0, 8),)),
        "up_bias": centred(key_of[13], (FF,), 0.5, 2.5, ((0, 8),)),
        "down_weight": centred(key_of[14], (FF, D), (FF // 2) ** -0.5, 0.15625, ((0, 8),)),
        "down_bias": centred(key_of[15], (D,), 0.5, 2.5, ((0, 8),)),
    }


@jax.custom_vjp
def low(v):
    return lax.optimization_barrier(v.astype(jnp.bfloat16)).astype(jnp.float32)

@jax.custom_vjp
def low_back(v):
    return v

def low_keep(v):
    return (low(v), None)

def low_pass(kept, grad):
    return (grad,)

def back_keep(v):
    return (v, None)

def back_low(kept, grad):
    return (low(grad),)
low.defvjp(low_keep, low_pass)
low_back.defvjp(back_keep, back_low)
EPSILON = 1e-06
NEGATIVE = -1e+30

def matmul(left, right):
    return jnp.dot(left, right, precision=lax.Precision.HIGHEST, preferred_element_type=jnp.float32)

def layer_norm(entries, norm_gain, norm_shift):
    centered = entries - lax.optimization_barrier(jnp.mean(entries, axis=-1, keepdims=True))
    spread = lax.optimization_barrier(jnp.mean(centered * centered, axis=-1, keepdims=True))
    return centered * lax.rsqrt(spread + EPSILON) * norm_gain + norm_shift

def valid_slots(crop_rows, crop_top):
    grid_row = jnp.arange(SLOTS, dtype=jnp.int32) // GRID
    upper = crop_top[:, None]
    return jnp.logical_and(grid_row[None, :] >= upper, grid_row[None, :] < upper + crop_rows[:, None])

def attend_group(pieces):
    queries, key_side, values, keep_slots = pieces
    scores = jnp.einsum('gihe,gjhe->ghij', queries, key_side, precision=lax.Precision.HIGHEST)
    scores = low_back(scores)
    masked = jnp.where(keep_slots[:, None, None, :], scores, NEGATIVE)
    highest = lax.optimization_barrier(jnp.max(masked, axis=-1, keepdims=True))
    powers = jnp.exp(masked - highest)
    probs = powers / lax.optimization_barrier(jnp.sum(powers, axis=-1, keepdims=True))
    return jnp.einsum('ghij,gjhe->gihe', low(probs), values, precision=lax.Precision.HIGHEST)

def block_forward(params, entries, keep_slots):
    attn_gain, attn_shift, heads_weight, heads_bias, proj_weight, proj_bias, mlp_gain, mlp_shift, up_weight, up_bias, down_weight, down_bias = params
    images = keep_slots.shape[0]
    group = math.gcd(images, max(1, 512 // SLOTS))
    count = images // group
    low_one = low(layer_norm(entries, attn_gain, attn_shift))
    projected = matmul(low_one, heads_weight)
    pre_query = low_back(projected[:, :D] + heads_bias[:D])
    pre_key = low_back(projected[:, D:2 * D])
    pre_value = low_back(projected[:, 2 * D:] + heads_bias[D:])
    queries = low(pre_query * (1.0 / math.sqrt(HEAD)))
    key_side = low(pre_key)
    values = low(pre_value)
    block_shape = (count, group, SLOTS, HEADS, HEAD)
    heads_out = lax.map(jax.checkpoint(attend_group), (queries.reshape(block_shape), key_side.reshape(block_shape), values.reshape(block_shape), keep_slots.reshape(count, group, SLOTS)))
    heads_out = low(low_back(heads_out.reshape(entries.shape)))
    resid = entries + low_back(matmul(heads_out, proj_weight) + proj_bias)
    low_two = low(layer_norm(resid, mlp_gain, mlp_shift))
    hidden = low_back(matmul(low_two, up_weight) + up_bias)
    active = low(jax.nn.gelu(hidden, approximate=True))
    result = resid + low_back(matmul(active, down_weight) + down_bias)
    return jnp.where(keep_slots.reshape(-1, 1), result, 0.0)

def reference(tokens, cotangent, crop_rows, crop_top, attn_gain, attn_shift, heads_weight, heads_bias, proj_weight, proj_bias, mlp_gain, mlp_shift, up_weight, up_bias, down_weight, down_bias):
    params = tuple((item.astype(jnp.float32) for item in (attn_gain, attn_shift, heads_weight, heads_bias, proj_weight, proj_bias, mlp_gain, mlp_shift, up_weight, up_bias, down_weight, down_bias)))
    keep_all = valid_slots(crop_rows, crop_top)
    block = math.gcd(IMAGES, 16)
    blocks = IMAGES // block
    token_blocks = tokens.reshape(blocks, block * SLOTS, D)
    cot_blocks = cotangent.reshape(blocks, block * SLOTS, D)
    keep_blocks = keep_all.reshape(blocks, block, SLOTS)

    def one_block(totals, pieces):
        token_part, cot_part, keep_part = pieces
        result, puller = jax.vjp(lambda a, b: block_forward(a, b, keep_part), params, token_part.astype(jnp.float32))
        param_grads, input_grad = puller(cot_part.astype(jnp.float32))
        totals = jax.tree.map(lambda a, b: a + b, totals, param_grads)
        return (totals, (result.astype(jnp.bfloat16), input_grad.astype(jnp.bfloat16)))
    zeros = jax.tree.map(jnp.zeros_like, params)
    totals, (outputs, input_grads) = lax.scan(one_block, zeros, (token_blocks, cot_blocks, keep_blocks))
    return (outputs.reshape(TOKENS, D), input_grads.reshape(TOKENS, D), totals[0], totals[1], totals[2], totals[3], totals[4], totals[5], totals[6], totals[7], totals[8], totals[9], totals[10], totals[11])
```

```python
import functools, math
import jax, jax.numpy as jnp
from jax import lax
from jax.experimental import pallas as pl
from jax.experimental.pallas import tpu as pltpu
from jax.sharding import PartitionSpec as P

HEADS = 16
EPS = 1e-6
NEG = -1e30
F32, BF16 = jnp.float32, jnp.bfloat16
NN = (((1,), (0,)), ((), ()))
NT = (((1,), (1,)), ((), ()))
TN = (((0,), (0,)), ((), ()))

def dot(a, b, kind):
    return lax.dot_general(a, b, kind, preferred_element_type=F32)

A_GAIN, A_SHIFT, P_BIAS, M_GAIN, M_SHIFT, D_BIAS, H_BIAS, U_BIAS = 0, 1, 2, 3, 4, 5, 6, 8
SQ = math.sqrt(2.0 / math.pi)

def norm_stats(x):
    mean = jnp.mean(x, axis=-1, keepdims=True)
    cen = x - mean
    var = jnp.mean(cen * cen, axis=-1, keepdims=True)
    rstd = lax.rsqrt(var + EPS)
    return cen * rstd, rstd

def loop(n, body):
    def step(i, c):
        body(i)
        return c
    lax.fori_loop(0, n, step, 0)

def ds(i, size):
    return pl.ds(pl.multiple_of(i * size, size), size)

def keep_rows(top_ref, rows_ref, img, shape):
    grid_row = lax.broadcasted_iota(jnp.int32, shape, 0)
    lo = top_ref[img] * 16
    hi = lo + rows_ref[img] * 16
    return jnp.logical_and(grid_row >= lo, grid_row < hi)

def head_spans(h):
    a, b = 48 * h, 48 * h + 48
    t0, t1 = a // 128, (b - 1) // 128
    if t0 == t1:
        return [(t0, a - 128 * t0, b - 128 * t0)]
    return [(t0, a - 128 * t0, 128), (t1, 0, b - 128 * t1)]

def head_tools(h, lane):
    spans = head_spans(h)
    def inside(lo, hi):
        return jnp.logical_and(lane >= lo, lane < hi)
    masks = [(t, inside(lo, hi)) for t, lo, hi in spans]
    mh = masks[0][1]
    for t, m in masks[1:]:
        mh = jnp.logical_or(mh, m)
    used = set()
    for t, lo, hi in spans:
        used |= set(range(lo, hi))
    free = [l for l in range(128) if l not in used][:4]
    def window(tiles):
        if len(spans) == 1:
            return tiles[spans[0][0]]
        return jnp.where(masks[0][1], tiles[spans[0][0]], tiles[spans[1][0]])
    return masks, mh, free, window

def split3(v):
    hi = v.astype(BF16)
    r = v - hi.astype(F32)
    mid = r.astype(BF16)
    lo = (r - mid.astype(F32)).astype(BF16)
    return hi, mid, lo

def attn_fwd(t, top_ref, rows_ref, qkv, qx, ho):
    img, half = t // 2, t % 2
    rows = ds(img, 256)
    def cols(base, j):
        return pl.ds(pl.multiple_of(half * 384 + base + 128 * j, 128), 128)
    q = [qkv[rows, cols(0, j)] for j in range(3)]
    k = [qkv[rows, cols(768, j)] for j in range(3)]
    v = [qkv[rows, cols(1536, j)] for j in range(3)]
    lane = lax.broadcasted_iota(jnp.int32, (256, 128), 1)
    bias = jnp.where(keep_rows(top_ref, rows_ref, img, (256, 128)), 0.0, NEG).astype(BF16)
    out = [jnp.zeros((256, 128), F32) for _ in range(3)]
    ones = jnp.ones((256, 128), BF16)
    zero, one = jnp.zeros((256, 128), BF16), jnp.ones((256, 128), BF16)
    for h in range(8):
        masks, mh, free, window = head_tools(h, lane)
        qw, kw, vw = window(q), window(k), window(v)
        qi = jnp.where(mh, qw, jnp.where(lane == free[0], one, zero))
        ki = jnp.where(lane == free[0], bias, kw)
        s = dot(qi, ki, NT)
        m = jnp.max(s, axis=1, keepdims=True)
        e = jnp.exp(s - m).astype(BF16)
        res = dot(e, jnp.concatenate([vw, ones], axis=1), NN)
        o, tot = res[:, :128], res[:, 128:]
        o = o / tot
        for j, mk in masks:
            out[j] = jnp.where(mk, o, out[j])
        lse = m + jnp.log(tot)
        hi, mid, lo = split3(-lse)
        ext = jnp.where(lane == free[1], hi, jnp.where(lane == free[2], mid, jnp.where(lane == free[3], lo, zero)))
        ext = jnp.where(lane == free[0], one, ext)
        qx[rows, pl.ds(pl.multiple_of(half * 1024 + 128 * h, 128), 128)] = jnp.where(mh, qw, ext)
    for j in range(3):
        ho[rows, cols(0, j)] = out[j].astype(BF16)

def attn_bwd(img, half, top_ref, rows_ref, qkv, qx, ho, gh, factor):
    rows = ds(img, 256)
    def cols(base, j):
        return pl.ds(pl.multiple_of(half * 384 + base + 128 * j, 128), 128)
    k = [qkv[rows, cols(768, j)] for j in range(3)]
    v = [qkv[rows, cols(1536, j)] for j in range(3)]
    o = [ho[rows, cols(0, j)] for j in range(3)]
    do = [gh[rows, cols(0, j)] for j in range(3)]
    lane = lax.broadcasted_iota(jnp.int32, (256, 128), 1)
    bias = jnp.where(keep_rows(top_ref, rows_ref, img, (256, 128)), 0.0, NEG).astype(BF16)
    zero, one = jnp.zeros((256, 128), BF16), jnp.ones((256, 128), BF16)
    dq = [jnp.zeros((256, 128), F32) for _ in range(3)]
    dk = [jnp.zeros((256, 128), F32) for _ in range(3)]
    dv = [jnp.zeros((256, 128), F32) for _ in range(3)]
    for h in range(8):
        masks, mh, free, window = head_tools(h, lane)
        kw, vw, ow, dow = window(k), window(v), window(o), window(do)
        qw = qx[rows, pl.ds(pl.multiple_of(half * 1024 + 128 * h, 128), 128)]
        ki = jnp.where(mh, kw, jnp.where(lane == free[0], bias, one))
        pt = jnp.exp(dot(ki, qw, NT))
        prod = jnp.where(mh, dow.astype(F32) * ow.astype(F32), 0.0)
        dd = jnp.broadcast_to(jnp.sum(prod, axis=1, keepdims=True), (256, 128))
        hi, mid, lo = split3(-dd)
        di = jnp.where(mh, dow, jnp.where(lane == free[1], hi, jnp.where(lane == free[2], mid, jnp.where(lane == free[3], lo, zero))))
        vi = jnp.where(mh, vw, one)
        dpt = dot(vi, di, NT)
        dst = (pt * dpt).astype(BF16)
        rv = dot(pt.astype(BF16), dow, NN)
        rk = dot(dst, qw, NN)
        rq = dot(dst, kw, TN) * factor
        for j, mk in masks:
            dq[j] = jnp.where(mk, rq, dq[j])
            dk[j] = jnp.where(mk, rk, dk[j])
            dv[j] = jnp.where(mk, rv, dv[j])
    for j in range(3):
        qkv[rows, cols(0, j)] = dq[j].astype(BF16)
        qkv[rows, cols(768, j)] = dk[j].astype(BF16)
        qkv[rows, cols(1536, j)] = dv[j].astype(BF16)

def st_norm1(tok, par, low1):
    def body(i):
        x = tok[ds(i, 256), :].astype(F32)
        xh, _ = norm_stats(x)
        low1[ds(i, 256), :] = (xh * par[A_GAIN:A_GAIN + 1, :] + par[A_SHIFT:A_SHIFT + 1, :]).astype(BF16)
    loop(4, body)

def st_mask(cot, top_ref, rows_ref, acc):
    def body(i):
        keep = keep_rows(top_ref, rows_ref, i, (256, 768))
        g = jnp.where(keep, cot[ds(i, 256), :].astype(F32), 0.0)
        acc[D_BIAS:D_BIAS + 1, :] += jnp.sum(g, axis=0, keepdims=True)
        cot[ds(i, 256), :] = g.astype(BF16)
    loop(4, body)

def st_qkv(n, low1, wqkv, par, qkv, factor):
    cols = slice(768 * n, 768 * n + 768)
    def body(i):
        p = dot(low1[ds(i, 256), :], wqkv[:, cols], NN)
        if n == 0:
            p = (p + par[H_BIAS:H_BIAS + 1, :]) * factor
        if n == 2:
            p = p + par[H_BIAS + 1:H_BIAS + 2, :]
        qkv[ds(i, 256), cols] = p.astype(BF16)
    loop(4, body)

def st_proj(ho, wp, tok, par, resid, low2):
    def body(i):
        rows = ds(i, 256)
        r = tok[rows, :].astype(F32) + (dot(ho[rows, :], wp[...], NN) + par[P_BIAS:P_BIAS + 1, :])
        resid[rows, :] = r
        xh, _ = norm_stats(r)
        low2[rows, :] = (xh * par[M_GAIN:M_GAIN + 1, :] + par[M_SHIFT:M_SHIFT + 1, :]).astype(BF16)
    loop(4, body)

def st_up(n, low2, wu, par, act, gp):
    cols = slice(768 * n, 768 * n + 768)
    def body(i):
        rows = ds(i, 256)
        z = dot(low2[rows, :], wu[:, cols], NN) + par[U_BIAS + n:U_BIAS + n + 1, :]
        z2 = z * z
        t = jnp.tanh(z * (SQ + (SQ * 0.044715) * z2))
        hz = 0.5 * z
        act[rows, cols] = (hz + hz * t).astype(BF16)
        gp[rows, cols] = (0.5 + 0.5 * t + hz * (1.0 - t * t) * (SQ + (3 * SQ * 0.044715) * z2)).astype(BF16)
    loop(4, body)

def st_down(act, wd, par, resid, top_ref, rows_ref, out):
    def body(i):
        rows = ds(i, 256)
        r = resid[rows, :] + (dot(act[rows, :], wd[...], NN) + par[D_BIAS:D_BIAS + 1, :])
        keep = keep_rows(top_ref, rows_ref, i, (256, 768))
        out[rows, :] = jnp.where(keep, r, 0.0).astype(BF16)
    loop(4, body)

def st_dwd(n, act, g, dwd):
    cols = slice(256 * n, 256 * n + 256)
    def body(i):
        dwd[ds(i, 768), cols] = dot(act[:, ds(i, 768)], g[:, cols], TN).astype(BF16)
    loop(4, body)

def st_gact(n, g, wd, gp, acc):
    cols = slice(768 * n, 768 * n + 768)
    def body(i):
        rows = ds(i, 256)
        ga = dot(g[rows, :], wd[cols, :], NT)
        gh = (ga * gp[rows, cols].astype(F32)).astype(BF16)
        acc[U_BIAS + n:U_BIAS + n + 1, :] += jnp.sum(gh.astype(F32), axis=0, keepdims=True)
        gp[rows, cols] = gh
    loop(4, body)

def st_dwu(n, low2, gh, dwu):
    cols = slice(768 * n, 768 * n + 768)
    def body(i):
        dwu[ds(i, 256), :] = dot(low2[:, ds(i, 256)], gh[:, cols], TN).astype(BF16)
    loop(3, body)

def st_gtwo(gh, wu, par, resid, g, acc, branch):
    def body(i):
        rows = ds(i, 256)
        gt = dot(gh[rows, :], wu[...], NT)
        xh, rstd = norm_stats(resid[rows, :])
        acc[M_GAIN:M_GAIN + 1, :] += jnp.sum(gt * xh, axis=0, keepdims=True)
        acc[M_SHIFT:M_SHIFT + 1, :] += jnp.sum(gt, axis=0, keepdims=True)
        u = gt * par[M_GAIN:M_GAIN + 1, :]
        m1 = jnp.mean(u, axis=1, keepdims=True)
        m2 = jnp.mean(u * xh, axis=1, keepdims=True)
        gr = g[rows, :].astype(F32) + (u - m1 - xh * m2) * rstd
        resid[rows, :] = gr
        b = gr.astype(BF16)
        acc[P_BIAS:P_BIAS + 1, :] += jnp.sum(b.astype(F32), axis=0, keepdims=True)
        branch[rows, :] = b
    loop(4, body)

def st_dwp(ho, branch, dwp):
    def body(i):
        dwp[ds(i, 256), :] = dot(ho[:, ds(i, 256)], branch[...], TN).astype(BF16)
    loop(3, body)

def st_gheads(branch, wp, gheads):
    def body(i):
        gheads[ds(i, 256), :] = dot(branch[ds(i, 256), :], wp[...], NT).astype(BF16)
    loop(4, body)

def st_hbias(qkv, acc):
    def body(i):
        rows = ds(i, 256)
        acc[H_BIAS:H_BIAS + 1, :] += jnp.sum(qkv[rows, 0:768].astype(F32), axis=0, keepdims=True)
        acc[H_BIAS + 1:H_BIAS + 2, :] += jnp.sum(qkv[rows, 1536:2304].astype(F32), axis=0, keepdims=True)
    loop(4, body)

def st_dwqkv(low1, dqkv, dw, ncol, base):
    def body(i):
        dw[ds(i, 256), base:base + ncol] = dot(low1[:, ds(i, 256)], dqkv[:, base:base + ncol], TN).astype(BF16)
    loop(3, body)

def st_gone(dqkv, wqkv, tok, par, gres, acc, out):
    def body(i):
        rows = ds(i, 256)
        go = dot(dqkv[rows, :], wqkv[...], NT)
        xh, rstd = norm_stats(tok[rows, :].astype(F32))
        acc[A_GAIN:A_GAIN + 1, :] += jnp.sum(go * xh, axis=0, keepdims=True)
        acc[A_SHIFT:A_SHIFT + 1, :] += jnp.sum(go, axis=0, keepdims=True)
        u = go * par[A_GAIN:A_GAIN + 1, :]
        m1 = jnp.mean(u, axis=1, keepdims=True)
        m2 = jnp.mean(u * xh, axis=1, keepdims=True)
        out[rows, :] = (gres[rows, :] + (u - m1 - xh * m2) * rstd).astype(BF16)
    loop(4, body)


def compute_kernel(top_ref, rows_ref, tok_h, cot_h, par, wqkv_h, wp_h, wu_h, wd_h,
                   out_h, tg_h, dwqkv_h, dwp_h, dwu_h, dwd_h, acc,
                   tok, cot, low1, qkv, qx, ho, resid, low2, act, gp, wqkv, wp, wu, wd, dwd, sems):
    factor = 1.0 / math.sqrt(768 // HEADS)
    cps = [pltpu.make_async_copy(s, d, sems.at[i]) for i, (s, d) in enumerate(
        ((tok_h, tok), (wqkv_h, wqkv), (wp_h, wp), (wu_h, wu), (cot_h, cot), (wd_h, wd)))]
    for c in cps:
        c.start()
    acc[...] = jnp.zeros_like(acc)
    cps[0].wait()
    st_norm1(tok, par, low1)
    cps[1].wait()
    for n in range(3):
        st_qkv(n, low1, wqkv, par, qkv, factor)
    loop(8, lambda t: attn_fwd(t, top_ref, rows_ref, qkv, qx, ho))
    cps[2].wait()
    st_proj(ho, wp, tok, par, resid, low2)
    cps[3].wait()
    for n in range(4):
        st_up(n, low2, wu, par, act, gp)
    cps[4].wait()
    st_mask(cot, top_ref, rows_ref, acc)
    for n in range(3):
        st_dwd(n, act, cot, dwd)
    cps[5].wait()
    stage = act.at[:, 0:768]
    gheads = act.at[:, 768:1536]
    st_down(act, wd, par, resid, top_ref, rows_ref, stage)
    o1 = pltpu.make_async_copy(stage, out_h, sems.at[6]); o1.start()
    o2 = pltpu.make_async_copy(dwd, dwd_h, sems.at[7]); o2.start()
    for n in range(4):
        st_gact(n, cot, wd, gp, acc)
    outs = [o2]
    for n in range(4):
        dst = wd.at[768 * n:768 * n + 768, :]
        st_dwu(n, low2, gp, dst)
        o = pltpu.make_async_copy(dst, dwu_h.at[n], sems.at[8 + n]); o.start()
        outs.append(o)
    st_gtwo(gp, wu, par, resid, cot, acc, low2)
    dwp = wu.at[:, 0:768]
    st_dwp(ho, low2, dwp)
    o = pltpu.make_async_copy(dwp, dwp_h, sems.at[12]); o.start()
    outs.append(o)
    st_gheads(low2, wp, gheads)
    dwqkv = wu.at[:, 768:3072]
    for half in range(2):
        loop(4, lambda img: attn_bwd(img, half, top_ref, rows_ref, qkv, qx, ho, gheads, factor))
    st_hbias(qkv, acc)
    for n in range(3):
        st_dwqkv(low1, qkv, dwqkv, 768, 768 * n)
    o = pltpu.make_async_copy(dwqkv, dwqkv_h, sems.at[13]); o.start()
    outs.append(o)
    o1.wait()
    st_gone(qkv, wqkv, tok, par, resid, acc, stage)
    o = pltpu.make_async_copy(stage, tg_h, sems.at[14]); o.start()
    outs.append(o)
    for o in outs:
        o.wait()


def compute_call(crop_top, crop_rows, tokens, cotangent, par, wqkv, wp, wu, wd):
    R = tokens.shape[0]
    sds = jax.ShapeDtypeStruct
    anyspec = pl.BlockSpec(memory_space=pl.ANY)
    v = pltpu.VMEM
    return pl.pallas_call(
        compute_kernel,
        out_shape=(sds((R, 768), BF16), sds((R, 768), BF16), sds((768, 2304), BF16), sds((768, 768), BF16),
                   sds((4, 768, 768), BF16), sds((3072, 768), BF16), sds((16, 768), F32)),
        in_specs=[pl.BlockSpec(memory_space=pltpu.SMEM)] * 2 + [anyspec] * 2 + [pl.BlockSpec(memory_space=v)] + [anyspec] * 4,
        out_specs=[anyspec] * 6 + [pl.BlockSpec(memory_space=v)],
        scratch_shapes=[v((R, 768), BF16), v((R, 768), BF16), v((R, 768), BF16), v((R, 2304), BF16), v((R, 2048), BF16),
                        v((R, 768), BF16), v((R, 768), F32), v((R, 768), BF16), v((R, 3072), BF16), v((R, 3072), BF16),
                        v((768, 2304), BF16), v((768, 768), BF16), v((768, 3072), BF16), v((3072, 768), BF16),
                        v((3072, 768), BF16), pltpu.SemaphoreType.DMA((16,))],
        compiler_params=pltpu.CompilerParams(vmem_limit_bytes=60 * 2**20),
        cost_estimate=pl.CostEstimate(flops=46 * 10**9, bytes_accessed=40 * 10**6, transcendentals=12 * 10**6),
    )(crop_top, crop_rows, tokens, cotangent, par, wqkv, wp, wu, wd)


def pack_small(ag, ash, hb, pb, mg, ms, ub, db):
    n = ag.shape[0]
    return jnp.concatenate(
        [jnp.stack([ag, ash, pb, mg, ms, db]), hb.reshape(2, n), ub.reshape(4, n), jnp.zeros((4, n), ag.dtype)]
    ).astype(F32)


def small_table(parts):
    s, _, n = parts.shape
    six = parts[:, :6].transpose(1, 0, 2).reshape(6, s * n)
    hb = parts[:, 6:8].reshape(2, s * n)
    ub = parts[:, 8:12].reshape(4, s * n)
    return jnp.concatenate([six, hb, ub, jnp.zeros((4, s * n), F32)])


def small_pieces(acc, s):
    n = acc.shape[1] // s
    six = acc[:6].reshape(6, s, n).transpose(1, 0, 2)
    hb = acc[6:8].reshape(s, 2, n)
    ub = acc[8:12].reshape(s, 4, n)
    return jnp.concatenate([six, hb, ub, jnp.zeros((s, 4, n), F32)], axis=1)


def shards(tokens, cotangent, crop_rows, crop_top, ag, ash, hw, hb, pw, pb, mg, ms, uw, ub, dw, db):
    def gather(a):
        return lax.all_gather(a, "fsdp", axis=0, tiled=True)

    def reduce(a):
        part = lax.psum_scatter(a.astype(BF16), "fsdp", scatter_dimension=0, tiled=True)
        return lax.psum(part, "dp").astype(F32)

    s = lax.axis_size("fsdp")
    par = small_table(lax.all_gather(pack_small(ag, ash, hb, pb, mg, ms, ub, db), "fsdp", axis=0))
    out, tg, dwqkv, dwp, dwu, dwd, acc = compute_call(
        crop_top, crop_rows, tokens, cotangent, par, gather(hw), gather(pw), gather(uw), gather(dw))
    dwu = dwu.transpose(1, 0, 2).reshape(uw.shape[0] * s, -1)
    small = small_pieces(acc, s)
    small = lax.psum(lax.psum_scatter(small, "fsdp", scatter_dimension=0, tiled=True), "dp")[0]
    return (out, tg, small[0], small[1], reduce(dwqkv), small[6:8].reshape(-1), reduce(dwp), small[2],
            small[3], small[4], reduce(dwu), small[8:12].reshape(-1), reduce(dwd), small[5])


def solution(mesh):
    row = P(("dp", "fsdp"), None)
    vec, mat = P("fsdp"), P("fsdp", None)
    return jax.shard_map(
        shards,
        mesh=mesh,
        in_specs=(row, row, P(("dp", "fsdp")), P(("dp", "fsdp")), vec, vec, mat, vec, mat, vec, vec, vec, mat, vec, mat, vec),
        out_specs=(row, row, vec, vec, mat, vec, mat, vec, vec, vec, mat, vec, mat, vec),
        check_vma=False,
    )
```

```python
import functools
import math

import jax
import jax.numpy as jnp
from jax import lax
from jax.experimental import pallas as pl
from jax.experimental.pallas import tpu as pltpu
from jax.sharding import PartitionSpec as P

HEADS = 16
EPS = 1e-6
NEG = -1e30
F32, BF16 = jnp.float32, jnp.bfloat16
NN = (((1,), (0,)), ((), ()))
NT = (((1,), (1,)), ((), ()))
TN = (((0,), (0,)), ((), ()))
SQ = math.sqrt(2.0 / math.pi)
CUBIC = 0.044715
MESH = pl.DeviceIdType.MESH

A_GAIN, A_SHIFT, P_BIAS, M_GAIN, M_SHIFT, D_BIAS, H_BIAS, U_BIAS = 0, 1, 2, 3, 4, 5, 6, 8


def dot(a, b, kind):
    return lax.dot_general(a, b, kind, preferred_element_type=F32)


def loop(n, body):
    def step(i, c):
        body(i)
        return c

    lax.fori_loop(0, n, step, 0)


def ds(i, size):
    return pl.ds(pl.multiple_of(i * size, size), size)


def normed(x):
    mean = jnp.mean(x, axis=-1, keepdims=True)
    cen = x - mean
    var = jnp.mean(cen * cen, axis=-1, keepdims=True)
    rstd = lax.rsqrt(var + EPS)
    return cen * rstd, rstd


def keep_mask(top, held, img, shape):
    row = lax.broadcasted_iota(jnp.int32, shape, 0)
    lo = top[img] * 16
    return jnp.logical_and(row >= lo, row < lo + held[img] * 16)


def head_tools(h, lane):
    a, b = 48 * h, 48 * h + 48
    t0, t1 = a // 128, (b - 1) // 128
    spans = [(t0, a - 128 * t0, min(b - 128 * t0, 128))]
    if t1 != t0:
        spans.append((t1, 0, b - 128 * t1))
    masks = [(t, jnp.logical_and(lane >= lo, lane < hi)) for t, lo, hi in spans]
    inside = functools.reduce(jnp.logical_or, [m for _, m in masks])
    used = {lane for _, lo, hi in spans for lane in range(lo, hi)}
    free = [i for i in range(128) if i not in used][:4]

    def window(tiles):
        if len(spans) == 1:
            return tiles[t0]
        return jnp.where(masks[0][1], tiles[t0], tiles[t1])

    return masks, inside, free, window


def split3(v):
    hi = v.astype(BF16)
    rest = v - hi.astype(F32)
    mid = rest.astype(BF16)
    return hi, mid, (rest - mid.astype(F32)).astype(BF16)


def spread3(lane, free, v, rest):
    hi, mid, lo = split3(v)
    return jnp.where(lane == free[1], hi, jnp.where(lane == free[2], mid, jnp.where(lane == free[3], lo, rest)))


def attn_forward(img, half, r):
    rows = ds(img, 256)
    cols = [slice(1152 * half + 128 * j, 1152 * half + 128 * j + 128) for j in range(9)]
    outs = [slice(384 * half + 128 * j, 384 * half + 128 * j + 128) for j in range(3)]
    q, k, v = ([r.qkv[rows, cols[3 * p + j]] for j in range(3)] for p in range(3))
    lane = lax.broadcasted_iota(jnp.int32, (256, 128), 1)
    bias = jnp.where(keep_mask(r.top, r.held, img, (256, 128)), 0.0, NEG).astype(BF16)
    zero, one = jnp.zeros((256, 128), BF16), jnp.ones((256, 128), BF16)
    out = [jnp.zeros((256, 128), F32) for _ in range(3)]
    for h in range(8):
        masks, inside, free, window = head_tools(h, lane)
        qw, kw, vw = window(q), window(k), window(v)
        qi = jnp.where(inside, qw, jnp.where(lane == free[0], one, zero))
        ki = jnp.where(lane == free[0], bias, kw)
        s = dot(qi, ki, NT)
        m = jnp.max(s, axis=1, keepdims=True)
        e = jnp.exp(s - m).astype(BF16)
        res = dot(e, jnp.concatenate([vw, one], axis=1), NN)
        tot = res[:, 128:]
        o = res[:, :128] / tot
        for j, mask in masks:
            out[j] = jnp.where(mask, o, out[j])
        ext = jnp.where(lane == free[0], one, spread3(lane, free, -(m + jnp.log(tot)), zero))
        c = 1024 * half + 128 * h
        r.qx[rows, c : c + 128] = jnp.where(inside, qw, ext)
    for j in range(3):
        r.ho[rows, outs[j]] = out[j].astype(BF16)


def attn_backward(img, half, r):
    rows = ds(img, 256)
    cols = [slice(1152 * half + 128 * j, 1152 * half + 128 * j + 128) for j in range(9)]
    outs = [slice(384 * half + 128 * j, 384 * half + 128 * j + 128) for j in range(3)]
    k, v = ([r.qkv[rows, cols[3 * p + j]] for j in range(3)] for p in (1, 2))
    o = [r.ho[rows, outs[j]] for j in range(3)]
    do = [r.gheads[rows, outs[j]] for j in range(3)]
    lane = lax.broadcasted_iota(jnp.int32, (256, 128), 1)
    bias = jnp.where(keep_mask(r.top, r.held, img, (256, 128)), 0.0, NEG).astype(BF16)
    zero, one = jnp.zeros((256, 128), BF16), jnp.ones((256, 128), BF16)
    dq, dk, dv = ([jnp.zeros((256, 128), F32) for _ in range(3)] for _ in range(3))
    for h in range(8):
        masks, inside, free, window = head_tools(h, lane)
        kw, vw, ow, dow = window(k), window(v), window(o), window(do)
        c = 1024 * half + 128 * h
        qw = r.qx[rows, c : c + 128]
        ki = jnp.where(inside, kw, jnp.where(lane == free[0], bias, one))
        pt = jnp.exp(dot(ki, qw, NT))
        prod = jnp.where(inside, dow.astype(F32) * ow.astype(F32), 0.0)
        inner = jnp.broadcast_to(jnp.sum(prod, axis=1, keepdims=True), (256, 128))
        di = jnp.where(inside, dow, spread3(lane, free, -inner, zero))
        dst = (pt * dot(jnp.where(inside, vw, one), di, NT)).astype(BF16)
        rv = dot(pt.astype(BF16), dow, NN)
        rk = dot(dst, qw, NN)
        rq = dot(dst, kw, TN) * r.factor
        for j, mask in masks:
            dq[j] = jnp.where(mask, rq, dq[j])
            dk[j] = jnp.where(mask, rk, dk[j])
            dv[j] = jnp.where(mask, rv, dv[j])
    for p, parts in enumerate((dq, dk, dv)):
        for j in range(3):
            r.qkv[rows, cols[3 * p + j]] = parts[j].astype(BF16)


def colsum(v):
    return jnp.sum(v, axis=0, keepdims=True)


def row(ref, i):
    return ref[i : i + 1, :]


def add_row(ref, i, v):
    ref[i : i + 1, :] += v


def stage_mask(r):
    def body(i):
        g = jnp.where(keep_mask(r.top, r.held, i, (256, 768)), r.tok[ds(i, 256), :].astype(F32), 0.0)
        add_row(r.acc, D_BIAS, colsum(g))
        r.tok[ds(i, 256), :] = g.astype(BF16)

    loop(4, body)


def stage_norm1(r):
    def body(i):
        xh, _ = normed(r.xin[ds(i, 256), :].astype(F32))
        r.low1[ds(i, 256), :] = (xh * row(r.par, A_GAIN) + row(r.par, A_SHIFT)).astype(BF16)

    loop(4, body)


def stage_qkv(half, r):
    cols = slice(1152 * half, 1152 * half + 1152)
    mine = slice(384 * half, 384 * half + 384)

    def body(i):
        w = r.wqkv[:, :, :, :, cols].reshape(768, 1152)
        p = dot(r.low1[ds(i, 256), :], w, NN)
        q = (p[:, :384] + r.par[H_BIAS : H_BIAS + 1, mine]) * r.factor
        v = p[:, 768:] + r.par[H_BIAS + 1 : H_BIAS + 2, mine]
        r.qkv[ds(i, 256), cols] = jnp.concatenate([q, p[:, 384:768], v], axis=1).astype(BF16)

    loop(4, body)


def stage_proj(r):
    def body(i):
        rows = ds(i, 256)
        w = r.wp[...].reshape(768, 768)
        x = r.xin[rows, :].astype(F32) + (dot(r.ho[rows, :], w, NN) + row(r.par, P_BIAS))
        r.resid[rows, :] = x
        xh, _ = normed(x)
        r.low2[rows, :] = (xh * row(r.par, M_GAIN) + row(r.par, M_SHIFT)).astype(BF16)

    loop(4, body)


def stage_up(n, r):
    cols = slice(768 * n, 768 * n + 768)

    def body(i):
        rows = ds(i, 256)
        z = dot(r.low2[rows, :], r.wu[:, :, :, :, cols].reshape(768, 768), NN) + row(r.par, U_BIAS + n)
        z2 = z * z
        t = jnp.tanh(z * (SQ + (SQ * CUBIC) * z2))
        hz = 0.5 * z
        r.act[rows, cols] = (hz + hz * t).astype(BF16)
        r.gp[rows, cols] = (0.5 + 0.5 * t + hz * (1.0 - t * t) * (SQ + (3 * SQ * CUBIC) * z2)).astype(BF16)

    loop(4, body)


def stage_down(r, first=0, count=4):
    def body(i):
        i = i + first
        rows = ds(i, 256)
        w = r.wd[...].reshape(3072, 768)
        x = r.resid[rows, :] + (dot(r.act[rows, :], w, NN) + row(r.par, D_BIAS))
        r.stage2[rows, :] = jnp.where(keep_mask(r.top, r.held, i, (256, 768)), x, 0.0).astype(BF16)

    loop(count, body)


def stage_dwd(n, r):
    cols = slice(256 * n, 256 * n + 256)

    def body(i):
        v = dot(r.act[:, ds(i, 768)], r.tok[:, cols], TN).astype(BF16)
        r.dwd[i // 2, i % 2, :, :, cols] = v.reshape(2, 384, 256)

    loop(4, body)


def stage_gact(n, r):
    cols = slice(768 * n, 768 * n + 768)
    y, x = n // 2, n % 2

    def body(i):
        rows = ds(i, 256)
        ga = dot(r.tok[rows, :], r.wd[y, x].reshape(768, 768), NT)
        gh = (ga * r.gp[rows, cols].astype(F32)).astype(BF16)
        add_row(r.acc, U_BIAS + n, colsum(gh.astype(F32)))
        r.gp[rows, cols] = gh

    loop(4, body)


def stage_dwu(n, r):
    cols = slice(768 * n, 768 * n + 768)

    def body(i):
        v = dot(r.low2[:, ds(i, 384)], r.gp[:, cols], TN).astype(BF16)
        r.dwu[i, :, :, n] = v.reshape(2, 2, 96, 768)

    loop(2, body)


def norm_back(grad, x, gain, acc, gain_row):
    xh, rstd = normed(x)
    add_row(acc, gain_row, colsum(grad * xh))
    add_row(acc, gain_row + 1, colsum(grad))
    u = grad * gain
    return (u - jnp.mean(u, axis=1, keepdims=True) - xh * jnp.mean(u * xh, axis=1, keepdims=True)) * rstd


def stage_gtwo(r, first=0, count=4):
    def body(i):
        rows = ds(i + first, 256)
        gt = dot(r.gp[rows, :], r.wu[...].reshape(768, 3072), NT)
        g = r.tok[rows, :].astype(F32) + norm_back(gt, r.resid[rows, :], row(r.par, M_GAIN), r.acc, M_GAIN)
        b = g.astype(BF16)
        add_row(r.acc, P_BIAS, colsum(b.astype(F32)))
        r.low2[rows, :] = b
        r.gp[rows, 0:768] = (g - b.astype(F32)).astype(BF16)

    loop(count, body)


def stage_dwp(r):
    def body(i):
        v = dot(r.ho[:, ds(i, 384)], r.low2[...], TN).astype(BF16)
        r.wu[i, :, :, :, 0:768] = v.reshape(2, 2, 96, 768)

    loop(2, body)


def stage_gheads(r):
    def body(i):
        r.gheads[ds(i, 256), :] = dot(r.low2[ds(i, 256), :], r.wp[...].reshape(768, 768), NT).astype(BF16)

    loop(4, body)


def stage_hbias(half, r):
    mine = slice(384 * half, 384 * half + 384)

    def body(i):
        d = r.qkv[ds(i, 256), 1152 * half : 1152 * half + 1152].astype(F32)
        r.acc[H_BIAS : H_BIAS + 1, mine] += colsum(d[:, :384])
        r.acc[H_BIAS + 1 : H_BIAS + 2, mine] += colsum(d[:, 768:])

    loop(4, body)


def stage_dwqkv(half, r):
    cols = slice(1152 * half, 1152 * half + 1152)
    into = slice(768 + 1152 * half, 1920 + 1152 * half)

    def body(i):
        v = dot(r.low1[:, ds(i, 384)], r.qkv[:, cols], TN).astype(BF16)
        r.wu[i, :, :, :, into] = v.reshape(2, 2, 96, 1152)

    loop(2, body)


def stage_gone(r, first=0, count=4):
    def body(i):
        rows = ds(i + first, 256)
        go = dot(r.qkv[rows, :], r.wqkv[...].reshape(768, 2304), NT)
        back = norm_back(go, r.xin[rows, :].astype(F32), row(r.par, A_GAIN), r.acc, A_GAIN)
        kept = r.low2[rows, :].astype(F32) + r.gp[rows, 0:768].astype(F32)
        r.stage[rows, :] = (kept + back).astype(BF16)

    loop(count, body)


def pieces(s):
    out = [(i, 96, i, 96 * s) for i in range(6)]
    out.append((6, 192, H_BIAS + s // 4, 192 * (s % 4)))
    out.append((7, 384, U_BIAS + s // 2, 384 * (s % 2)))
    return out


def spread_small(src, par):
    for s in range(8):
        for i, n, t, c in pieces(s):
            par[t : t + 1, c : c + n] = src[s // 4, s // 2 % 2, s % 2, i : i + 1, 0:n]


def gather_small(acc, dst):
    for s in range(8):
        dst[s // 4, s // 2 % 2, s % 2] = jnp.zeros((8, 384), F32)
        for i, n, t, c in pieces(s):
            dst[s // 4, s // 2 % 2, s % 2, i : i + 1, 0:n] = acc[t : t + 1, c : c + n]


class Links:
    def __init__(self, send, recv):
        z, f = lax.axis_index("dp"), lax.axis_index("fsdp")
        self.y, self.x, self.c = lax.div(f, 4), lax.rem(lax.div(f, 2), 2), lax.rem(f, 2)
        y, x, c = self.y, self.x, self.c
        self.z = z
        self.e = lax.rem(lax.div(z + 1, 2), 2)
        e = self.e

        def at(yy, xx, cc):
            return (z, 4 * yy + 2 * xx + cc)

        self.nx, self.ny, self.nd, self.nc = at(y, 1 - x, c), at(1 - y, x, c), at(1 - y, 1 - x, c), at(y, x, 1 - c)
        self.nz, self.nm, self.nw = (z + 1 - 2 * lax.rem(z, 2), f), (3 - z, f), (lax.rem(z + 2, 4), f)
        self.p1 = (y + e * (1 - 2 * y), x + (1 - e) * (1 - 2 * x))
        self.p2 = (y + (1 - e) * (1 - 2 * y), x + e * (1 - 2 * x))
        self.d1, self.d2 = at(*self.p1, c), at(*self.p2, c)
        self.send, self.recv, self.count = send, recv, 0
        self.started = []

    def greet(self):
        barrier = pltpu.get_barrier_semaphore()
        partners = (self.nx, self.ny, self.nd, self.nc, self.nz, self.nm, self.nw)
        for p in partners:
            pl.semaphore_signal(barrier, inc=1, device_id=p, device_id_type=MESH)
        pl.semaphore_wait(barrier, len(partners))

    def copy(self, src, dst, to):
        i = self.count
        self.count += 1
        c = pltpu.make_async_remote_copy(
            src_ref=src, dst_ref=dst, send_sem=self.send.at[i], recv_sem=self.recv.at[i], device_id=to, device_id_type=MESH
        )
        c.start()
        self.started.append(c)
        return c

    def sent(self, c):
        c.wait_send()
        self.started = [other for other in self.started if other is not c]

    def flush(self):
        for c in self.started:
            c.wait_send()
        self.started = []


def half_rows(rows, h):
    n = rows // 2
    return pl.ds(pl.multiple_of(h * n, n), n)


class Direct:
    def __init__(self, links, view, rows):
        l = self.l = links
        self.every = view(slice(0, 2), slice(0, 2), l.c, slice(0, rows))
        mine = view(l.y, l.x, l.c, slice(0, rows))
        self.hops = [l.copy(mine, mine, to) for to in (l.nx, l.ny, l.nd)]

    def share(self):
        for cp in self.hops:
            cp.wait_recv()
        self.core = self.l.copy(self.every, self.every, self.l.nc)

    def finish(self):
        self.core.wait_recv()


class Relay:
    def __init__(self, links, view, rows):
        l = self.l = links
        self.view, self.rows = view, rows
        mine = view(l.y, l.x, l.c, slice(0, rows))
        self.hops = [l.copy(mine, mine, to) for to in (l.nx, l.ny)]

    def turn(self):
        l, view, n = self.l, self.view, self.rows // 2
        for cp in self.hops:
            cp.wait_recv()
        one = view(l.y, 1 - l.x, l.c, slice(0, n))
        two = view(1 - l.y, l.x, l.c, slice(n, 2 * n))
        self.hops = [l.copy(one, one, l.ny), l.copy(two, two, l.nx)]

    def share(self):
        l = self.l
        for cp in self.hops:
            cp.wait_recv()
        every = self.view(slice(0, 2), slice(0, 2), l.c, slice(0, self.rows))
        self.core = l.copy(every, every, l.nc)

    def finish(self):
        self.core.wait_recv()


class Gather:
    def __init__(self, links, chunks):
        self.l, self.chunks, self.done, self.state = links, chunks, 0, [dict() for _ in chunks]

    def first(self, i):
        if i >= len(self.chunks):
            return
        l, (view, rows), st = self.l, self.chunks[i], self.state[i]
        full = view(l.y, l.x, l.c, slice(0, rows))
        st["p"] = l.copy(full, full, l.d1)
        part = view(l.y, l.x, l.c, slice(0, rows // 2))
        st["q"] = l.copy(part, part, l.d2)

    def at(self, i):
        if 0 <= i < len(self.chunks):
            return [(self.state[i], *self.chunks[i])]
        return []

    def tick(self):
        l, i = self.l, self.done
        self.done += 1
        for st, view, rows in self.at(i - 5):
            st["c"].wait_recv()
        for st, view, rows in self.at(i - 4):
            st["zp"].wait_recv()
            st["zd"].wait_recv()
            every = view(slice(0, 2), slice(0, 2), l.c, slice(0, rows))
            st["c"] = l.copy(every, every, l.nc)
        for st, view, rows in self.at(i - 2):
            st["q"].wait_recv()
            st["d"].wait_recv()
            part = view(1 - l.y, 1 - l.x, l.c, half_rows(rows, l.e))
            st["zd"] = l.copy(part, part, l.nz)
        for st, view, rows in self.at(i):
            st["p"].wait_recv()
            part = view(*l.p1, l.c, half_rows(rows, l.e))
            st["d"] = l.copy(part, part, l.d2)
            part = view(*l.p1, l.c, half_rows(rows, 1))
            st["zp"] = l.copy(part, part, l.nz)
        self.first(i + 2)

    def need(self, i):
        while self.done < i + 6:
            self.tick()

    def more(self):
        if self.done < len(self.chunks) + 5:
            self.tick()


class Reduce:
    def __init__(self, links):
        self.l, self.flying = links, []

    def push(self, view, rows, bufs, finish, advance=True):
        if advance:
            self.advance()
        st = dict(view=view, rows=rows, bufs=bufs, finish=finish, step=0)
        l = self.l
        st["c"] = l.copy(view(slice(0, 2), slice(0, 2), 1 - l.c, slice(0, rows)), bufs["c"](), l.nc)
        self.flying.append(st)

    def advance(self):
        for st in list(self.flying):
            st["step"] += 1
            getattr(self, "step%d" % st["step"])(st)

    def step1(self, st):
        l, view, b, n = self.l, st["view"], st["bufs"], st["rows"]
        st["c"].wait_recv()
        got = b["c"]()
        for y in range(2):
            for x in range(2):
                mine = view(y, x, l.c, slice(0, n))
                mine[...] += got[y, x]
        h0, h1 = slice(0, n // 2), slice(n // 2, n)
        st["x"] = l.copy(view(slice(0, 2), 1 - l.x, l.c, h0), b["x"](0), l.nx)
        st["y"] = l.copy(view(1 - l.y, slice(0, 2), l.c, h1), b["x"](1), l.ny)

    def step2(self, st):
        l, view, b, n = self.l, st["view"], st["bufs"], st["rows"]
        h0, h1 = slice(0, n // 2), slice(n // 2, n)
        st["x"].wait_recv()
        st["y"].wait_recv()
        for i in range(2):
            mine = view(i, l.x, l.c, h0)
            mine[...] += b["x"](0)[i]
            mine = view(l.y, i, l.c, h1)
            mine[...] += b["x"](1)[i]
        st["x"] = l.copy(view(1 - l.y, l.x, l.c, h0), b["y"](0), l.ny)
        st["y"] = l.copy(view(l.y, 1 - l.x, l.c, h1), b["y"](1), l.nx)

    def step3(self, st):
        l, view, b, n = self.l, st["view"], st["bufs"], st["rows"]
        st["x"].wait_recv()
        st["y"].wait_recv()
        mine = view(l.y, l.x, l.c, slice(0, n // 2))
        mine[...] += b["y"](0)[...]
        mine = view(l.y, l.x, l.c, slice(n // 2, n))
        mine[...] += b["y"](1)[...]
        st["z"] = l.copy(view(l.y, l.x, l.c, half_rows(n, 1 - l.e)), b["z"](0), l.nz)

    def step4(self, st):
        l, view, b, n = self.l, st["view"], st["bufs"], st["rows"]
        st["z"].wait_recv()
        l.sent(st["z"])
        mine = view(l.y, l.x, l.c, half_rows(n, l.e))
        mine[...] += b["z"](0)[...]
        st["z"] = l.copy(mine, b["z"](1), l.nm)

    def step5(self, st):
        l, view, b, n = self.l, st["view"], st["bufs"], st["rows"]
        st["z"].wait_recv()
        l.sent(st["z"])
        mine = view(l.y, l.x, l.c, half_rows(n, l.e))
        mine[...] += b["z"](1)[...]
        st["z"] = l.copy(mine, b["z"](2), l.nz)

    def step6(self, st):
        l = self.l
        st["z"].wait_recv()
        st["view"](l.y, l.x, l.c, half_rows(st["rows"], 1 - l.e))[...] = st["bufs"]["z"](2)[...]
        st["finish"](st["view"](l.y, l.x, l.c, slice(0, st["rows"])))
        self.flying = [other for other in self.flying if other is not st]


class ReduceSmall:
    def __init__(self, links, r):
        l = self.l = links
        self.r = r
        self.hops = [l.copy(r.smallg.at[:, :, 1 - l.c], r.cs, l.nc)]

    def wait(self):
        for cp in self.hops:
            cp.wait_recv()

    def plane(self):
        l, r = self.l, self.r
        self.wait()
        for y in range(2):
            for x in range(2):
                r.smallg[y, x, l.c] += r.cs[y, x]
        to = ((l.y, 1 - l.x, l.nx), (1 - l.y, l.x, l.ny), (1 - l.y, 1 - l.x, l.nd))
        self.hops = [l.copy(r.smallg.at[y, x, l.c], r.xs.at[i], p) for i, (y, x, p) in enumerate(to)]

    def replicas(self):
        l, r = self.l, self.r
        self.wait()
        r.zs[l.z] = r.smallg[l.y, l.x, l.c] + r.xs[0] + r.xs[1] + r.xs[2]
        self.hops = [l.copy(r.zs.at[l.z], r.zs.at[l.z], p) for p in (l.nz, l.nm, l.nw)]

    def total(self):
        r = self.r
        self.wait()
        r.fs[...] = (r.zs[0] + r.zs[1]) + (r.zs[2] + r.zs[3])


class Refs:
    pass


NAMES = (
    "top", "held", "tok_h", "cot_h", "small_h", "wqkv_h", "wp_h", "wu_h", "wd_h",
    "out_h", "tg_h", "fq_h", "fp_h", "fu_h", "fd_h", "fs",
    "tok", "low1", "qkv", "qx", "ho", "resid", "low2", "act", "gp", "wqkv", "wp", "wu", "wd", "dwd", "dwu",
    "small", "par", "acc", "smallg", "cd", "xd", "yd", "zd", "cq", "xq", "yq", "zq", "cs", "xs", "zs",
    "local", "send", "recv",
)


def set_views(r):
    r.factor = 1.0 / math.sqrt(768 // HEADS)
    r.xin = r.tok
    r.stage, r.gheads, r.stage2 = (r.gp.at[:, 768 * i : 768 * i + 768] for i in (1, 2, 3))


def fused_kernel(*args):
    r = Refs()
    for name, ref in zip(NAMES, args, strict=True):
        setattr(r, name, ref)
    set_views(r)
    l = Links(r.send, r.recv)
    y, x, c = l.y, l.x, l.c
    locals_ = []

    def local(src, dst):
        i = len(locals_)
        cp = pltpu.make_async_copy(src, dst, r.local.at[i])
        cp.start()
        locals_.append(cp)
        return cp

    def qcols(half, part):
        a, b = 768 * part + 384 * half, 1152 * half + 384 * part
        return slice(a, a + 384), slice(b, b + 384)

    load_small = local(r.small_h, r.small.at[y, x, c])
    load_q = [
        [local(r.wqkv_h.at[:, a], r.wqkv.at[y, x, c, :, b]) for a, b in (qcols(half, part) for part in range(3))]
        for half in range(2)
    ]
    load_tok = local(r.tok_h, r.tok)
    load_w = [local(r.wp_h, r.wp.at[y, x, c]), local(r.wu_h, r.wu.at[y, x, c]), local(r.wd_h, r.wd.at[y, x, c])]
    l.greet()

    def qview(half):
        k = slice(1152 * half, 1152 * half + 1152)
        return lambda a, b, d, s: r.wqkv.at[a, b, d, s, k]

    def uview(n):
        k = slice(768 * n, 768 * n + 768)
        return lambda a, b, d, s: r.wu.at[a, b, d, s, k]

    chunks = [(lambda a, b, d, s: r.wp.at[a, b, d, s, :], 96)]
    chunks += [(uview(n), 96) for n in range(4)]
    chunks += [(functools.partial(lambda k, a, b, d, s: r.wd.at[a, b, d, k, s, :], n), 96) for n in range(4)]
    load_small.wait()
    g_small = Direct(l, lambda a, b, d, s: r.small.at[a, b, d, s, :], 8)
    for cp in load_q[0]:
        cp.wait()
    g_first = Direct(l, qview(0), 96)
    for cp in load_q[1] + load_w + [load_tok]:
        cp.wait()
    g_second = Relay(l, qview(1), 96)
    g = Gather(l, chunks)
    r.acc[...] = jnp.zeros_like(r.acc)
    g_small.share()
    g_first.share()
    g.first(0)
    g_small.finish()
    spread_small(r.small, r.par)
    stage_norm1(r)
    g_first.finish()

    stage_qkv(0, r)
    g_second.turn()
    g.first(1)
    loop(4, lambda i: attn_forward(i, 0, r))
    g_second.share()
    g.more()
    g_second.finish()
    stage_qkv(1, r)
    g.more()
    loop(2, lambda i: attn_forward(i, 1, r))
    g.more()
    loop(2, lambda i: attn_forward(i + 2, 1, r))
    g.more()
    g.more()
    g.need(0)
    stage_proj(r)
    load_cot = local(r.cot_h, r.tok)
    for n in range(4):
        g.need(1 + n)
        stage_up(n, r)
    g.more()

    red = Reduce(l)

    def fam_d(s):
        return dict(c=lambda: r.cd.at[s], x=lambda t: r.xd.at[s, t], y=lambda t: r.yd.at[s, t], z=lambda t: r.zd.at[s, t])

    def fam_q(s, k):
        return dict(
            c=lambda: r.cq.at[s, :, :, :, k], x=lambda t: r.xq.at[s, t, :, :, k],
            y=lambda t: r.yq.at[s, t, :, k], z=lambda t: r.zq.at[s, t, :, k],
        )

    finals = []

    def to(ref):
        return lambda mine: finals.append(local(mine, ref))

    def push_d(n):
        k = slice(256 * n, 256 * n + 256)
        red.push(lambda a, b, d, s: r.dwd.at[a, b, d, s, k], 384, fam_d(n % 2), to(r.fd_h.at[:, k]))

    def push_u(n):
        k = slice(768 * n, 768 * n + 768)
        red.push(lambda a, b, d, s: r.dwu.at[a, b, d, n, s, :], 96, fam_q(n % 2, slice(0, 768)), to(r.fu_h.at[:, k]))

    def push_p():
        red.push(lambda a, b, d, s: r.wu.at[a, b, d, s, 0:768], 96, fam_q(0, slice(0, 768)), to(r.fp_h))

    def push_q(half, part, advance):
        a, b = qcols(half, part)
        k = slice(768 + b.start, 768 + b.stop)
        bufs = fam_q(1 - half, slice(384 * part, 384 * part + 384))
        red.push(lambda i, j, d, s: r.wu.at[i, j, d, s, k], 96, bufs, to(r.fq_h.at[:, a]), advance)

    load_cot.wait()
    stage_mask(r)
    stage_dwd(0, r)
    g.more()
    push_d(0)
    stage_dwd(1, r)
    g.more()
    push_d(1)
    stage_dwd(2, r)
    g.need(8)
    stage_gact(0, r)
    stage_gact(1, r)
    push_d(2)
    stage_gact(2, r)
    stage_gact(3, r)
    l.flush()
    stage_dwu(0, r)
    stage_dwu(1, r)
    push_u(0)
    stage_dwu(2, r)
    stage_dwu(3, r)
    stage_gtwo(r, 0, 2)
    push_u(1)
    stage_gtwo(r, 2, 2)
    load_tok = local(r.tok_h, r.tok)
    stage_dwp(r)
    push_u(2)
    stage_gheads(r)
    loop(1, lambda i: attn_backward(i, 0, r))
    push_u(3)
    loop(2, lambda i: attn_backward(i + 1, 0, r))
    push_p()
    loop(1, lambda i: attn_backward(i + 3, 0, r))
    stage_dwqkv(0, r)
    for part in range(3):
        push_q(0, part, part == 0)
    stage_hbias(0, r)
    loop(2, lambda i: attn_backward(i, 1, r))
    red.advance()
    loop(2, lambda i: attn_backward(i + 2, 1, r))
    stage_dwqkv(1, r)
    for part in range(3):
        push_q(1, part, part == 0)
    stage_hbias(1, r)
    load_tok.wait()
    stage_gone(r, 0, 2)
    red.advance()
    stage_gone(r, 2, 2)
    store_tg = local(r.stage, r.tg_h)
    gather_small(r.acc, r.smallg)
    rs = ReduceSmall(l, r)
    stage_down(r, 0, 2)
    rs.plane()
    red.advance()
    stage_down(r, 2, 2)
    store_out = local(r.stage2, r.out_h)
    rs.replicas()
    red.advance()
    rs.total()
    while red.flying:
        red.advance()
    l.flush()
    store_tg.wait()
    store_out.wait()
    for cp in finals:
        cp.wait()


def fused_call(top, held, tokens, cotangent, small, wqkv, wp, wu, wd):
    rows = tokens.shape[0]
    sds = jax.ShapeDtypeStruct
    v = pltpu.VMEM
    hbm = pl.BlockSpec(memory_space=pl.ANY)
    dma = pltpu.SemaphoreType.DMA
    b = lambda *s: v(s, BF16)
    f = lambda *s: v(s, F32)
    return pl.pallas_call(
        fused_kernel,
        out_shape=(
            sds((rows, 768), BF16), sds((rows, 768), BF16), sds((96, 2304), BF16), sds((96, 768), BF16),
            sds((96, 3072), BF16), sds((384, 768), BF16), sds((8, 384), F32),
        ),
        in_specs=[pl.BlockSpec(memory_space=pltpu.SMEM)] * 2 + [hbm] * 7,
        out_specs=[hbm] * 6 + [pl.BlockSpec(memory_space=v)],
        scratch_shapes=[
            b(rows, 768), b(rows, 768), b(rows, 2304), b(rows, 2048), b(rows, 768), f(rows, 768), b(rows, 768),
            b(rows, 3072), b(rows, 3072),
            b(2, 2, 2, 96, 2304), b(2, 2, 2, 96, 768), b(2, 2, 2, 96, 3072), b(2, 2, 2, 4, 96, 768), b(2, 2, 2, 384, 768),
            b(2, 2, 2, 4, 96, 768),
            f(2, 2, 2, 8, 384), f(16, 768), f(16, 768), f(2, 2, 2, 8, 384),
            b(2, 2, 2, 384, 256), b(2, 2, 2, 192, 256), b(2, 2, 192, 256), b(2, 3, 192, 256),
            b(2, 2, 2, 96, 1152), b(2, 2, 2, 48, 1152), b(2, 2, 48, 1152), b(2, 3, 48, 1152),
            f(2, 2, 8, 384), f(3, 8, 384), f(4, 8, 384),
            dma((40,)), dma((200,)), dma((200,)),
        ],
        compiler_params=pltpu.CompilerParams(collective_id=0, has_side_effects=True, vmem_limit_bytes=64 * 2**20),
        cost_estimate=pl.CostEstimate(flops=46 * 10**9, bytes_accessed=20 * 10**6, transcendentals=12 * 10**6),
    )(top, held, tokens, cotangent, small, wqkv, wp, wu, wd)


PLAIN = (
    "top", "held", "tok_h", "cot_h", "par", "wqkv_h", "wp_h", "wu_h", "wd_h", "out_h", "tg_h", "gq_h", "gp_h", "gu_h",
    "gd_h", "acc", "xin", "tok", "low1", "qkv", "qx", "ho", "resid", "low2", "act", "gp", "wqkv", "wp", "wu", "wd",
    "dwd", "dwu", "local",
)


def plain_kernel(*args):
    r = Refs()
    for name, ref in zip(PLAIN, args, strict=True):
        setattr(r, name, ref)
    xin = r.xin
    set_views(r)
    r.xin = xin

    def every(pairs):
        copies = [pltpu.make_async_copy(src, dst, r.local.at[i]) for i, (src, dst) in enumerate(pairs)]
        for cp in copies:
            cp.start()
        for cp in copies:
            cp.wait()

    def mixed(ref, k):
        return ref.at[:, :, :, :, k]

    blocks = [(p, h, slice(768 * p + 384 * h, 768 * p + 384 * h + 384), 1152 * h + 384 * p) for h in range(2) for p in range(3)]
    every(
        [(r.tok_h, r.xin), (r.cot_h, r.tok), (r.wp_h, r.wp), (r.wu_h, r.wu), (r.wd_h, r.wd)]
        + [(mixed(r.wqkv_h, a), mixed(r.wqkv, slice(b, b + 384))) for _, _, a, b in blocks]
    )
    r.acc[...] = jnp.zeros_like(r.acc)
    stage_mask(r)
    stage_norm1(r)
    for half in range(2):
        stage_qkv(half, r)
        loop(4, lambda i: attn_forward(i, half, r))
    stage_proj(r)
    for n in range(4):
        stage_up(n, r)
    for n in range(3):
        stage_dwd(n, r)
    for n in range(4):
        stage_gact(n, r)
    for n in range(4):
        stage_dwu(n, r)
    stage_gtwo(r)
    stage_dwp(r)
    stage_gheads(r)
    for half in range(2):
        loop(4, lambda i: attn_backward(i, half, r))
        stage_dwqkv(half, r)
        stage_hbias(half, r)
    stage_gone(r)
    stage_down(r)
    every(
        [(r.stage, r.tg_h), (r.stage2, r.out_h), (r.dwd, r.gd_h), (mixed(r.wu, slice(0, 768)), r.gp_h)]
        + [(r.dwu.at[:, :, :, n], mixed(r.gu_h, slice(768 * n, 768 * n + 768))) for n in range(4)]
        + [(mixed(r.wu, slice(768 + b, 1152 + b)), mixed(r.gq_h, a)) for _, _, a, b in blocks]
    )


def plain_call(top, held, tokens, cotangent, par, wqkv, wp, wu, wd):
    rows = tokens.shape[0]
    sds = jax.ShapeDtypeStruct
    v = pltpu.VMEM
    hbm = pl.BlockSpec(memory_space=pl.ANY)
    b = lambda *s: v(s, BF16)
    f = lambda *s: v(s, F32)
    o = lambda *s: sds((2, 2, 2) + s, BF16)
    return pl.pallas_call(
        plain_kernel,
        out_shape=(
            sds((rows, 768), BF16), sds((rows, 768), BF16), o(96, 2304), o(96, 768), o(96, 3072), o(384, 768),
            sds((16, 768), F32),
        ),
        in_specs=[pl.BlockSpec(memory_space=pltpu.SMEM)] * 2 + [hbm] * 2 + [pl.BlockSpec(memory_space=v)] + [hbm] * 4,
        out_specs=[hbm] * 6 + [pl.BlockSpec(memory_space=v)],
        scratch_shapes=[
            b(rows, 768), b(rows, 768), b(rows, 768), b(rows, 2304), b(rows, 2048), b(rows, 768), f(rows, 768), b(rows, 768),
            b(rows, 3072), b(rows, 3072),
            b(2, 2, 2, 96, 2304), b(2, 2, 2, 96, 768), b(2, 2, 2, 96, 3072), b(2, 2, 2, 4, 96, 768), b(2, 2, 2, 384, 768),
            b(2, 2, 2, 4, 96, 768), pltpu.SemaphoreType.DMA((16,)),
        ],
        compiler_params=pltpu.CompilerParams(vmem_limit_bytes=64 * 2**20),
        cost_estimate=pl.CostEstimate(flops=46 * 10**9, bytes_accessed=40 * 10**6, transcendentals=12 * 10**6),
    )(top, held, tokens, cotangent, par, wqkv, wp, wu, wd)


def pack_small(*vectors):
    n = max(v.shape[0] for v in vectors)
    return jnp.stack([jnp.pad(v.astype(F32), (0, n - v.shape[0])) for v in vectors])


def fused_shards(tokens, cotangent, crop_rows, crop_top, ag, ash, hw, hb, pw, pb, mg, ms, uw, ub, dw, db):
    small = pack_small(ag, ash, pb, mg, ms, db, hb, ub)
    out, tg, fq, fp, fu, fd, fs = fused_call(
        crop_top, crop_rows, tokens, cotangent, small, hw, pw, uw, dw.reshape(4, 96, 768)
    )
    s = [fs[i, :96] for i in range(6)] + [fs[6, :192], fs[7]]
    return (
        out, tg, s[0], s[1], fq.astype(F32), s[6], fp.astype(F32), s[2],
        s[3], s[4], fu.astype(F32), s[7], fd.astype(F32), s[5],
    )


def plain_shards(tokens, cotangent, crop_rows, crop_top, ag, ash, hw, hb, pw, pb, mg, ms, uw, ub, dw, db):
    size = lax.axis_size("fsdp")

    def gather(a, shape):
        return lax.all_gather(a, "fsdp", axis=0, tiled=True).reshape((2, 2, 2) + shape)

    def reduce(a):
        part = a.reshape((-1, a.shape[-1]))
        part = lax.psum_scatter(part, "fsdp", scatter_dimension=0, tiled=True)
        return lax.psum(part, "dp")

    n = ag.shape[0]
    small = lax.all_gather(pack_small(ag, ash, pb, mg, ms, db, hb, ub), "fsdp", axis=0)
    six = small[:, :6, :n].transpose(1, 0, 2).reshape(6, -1)
    par = jnp.concatenate([six, small[:, 6, : 2 * n].reshape(2, -1), small[:, 7].reshape(4, -1), jnp.zeros((4, 768), F32)])
    out, tg, gq, gp, gu, gd, acc = plain_call(
        crop_top, crop_rows, tokens, cotangent, par, gather(hw, (96, 2304)), gather(pw, (96, 768)),
        gather(uw, (96, 3072)), gather(dw, (4, 96, 768)),
    )
    six = acc[:6].reshape(6, size, -1).transpose(1, 0, 2)
    pieces = jnp.concatenate([six, acc[6:8].reshape(size, 2, -1), acc[8:12].reshape(size, 4, -1)], axis=1)
    s = lax.psum(lax.psum_scatter(pieces, "fsdp", scatter_dimension=0, tiled=True), "dp")[0]
    gq, gp, gu, gd = (reduce(a).astype(F32) for a in (gq, gp, gu, gd))
    return (
        out, tg, s[0], s[1], gq, s[6:8].reshape(-1), gp, s[2],
        s[3], s[4], gu, s[8:12].reshape(-1), gd, s[5],
    )


def solution(mesh):
    rows = P(("dp", "fsdp"), None)
    vec, mat = P("fsdp"), P("fsdp", None)
    fits = mesh.shape["dp"] == 4 and mesh.shape["fsdp"] == 8
    return jax.shard_map(
        fused_shards if fits else plain_shards,
        mesh=mesh,
        in_specs=(rows, rows, P(("dp", "fsdp")), P(("dp", "fsdp")), vec, vec, mat, vec, mat, vec, vec, vec, mat, vec, mat, vec),
        out_specs=(rows, rows, vec, vec, mat, vec, mat, vec, vec, vec, mat, vec, mat, vec),
        check_vma=False,
    )
```

```python
import functools
import math

import jax
import jax.numpy as jnp
from jax import lax
from jax.experimental import pallas as pl
from jax.experimental.pallas import tpu as pltpu
from jax.sharding import PartitionSpec as P

HEADS = 16
EPS = 1e-6
NEG = -1e30
F32, BF16 = jnp.float32, jnp.bfloat16
NN = (((1,), (0,)), ((), ()))
NT = (((1,), (1,)), ((), ()))
TN = (((0,), (0,)), ((), ()))
SQ = math.sqrt(2.0 / math.pi)
CUBIC = 0.044715
MESH = pl.DeviceIdType.MESH

A_GAIN, A_SHIFT, P_BIAS, M_GAIN, M_SHIFT, D_BIAS, H_BIAS, U_BIAS = 0, 1, 2, 3, 4, 5, 6, 8


def dot(a, b, kind):
    return lax.dot_general(a, b, kind, preferred_element_type=F32)


def loop(n, body):
    def step(i, c):
        body(i)
        return c

    lax.fori_loop(0, n, step, 0, unroll=min(n,4))


def ds(i, size):
    return pl.ds(pl.multiple_of(i * size, size), size)


def normed(x):
    mean = jnp.mean(x, axis=-1, keepdims=True)
    cen = x - mean
    var = jnp.mean(cen * cen, axis=-1, keepdims=True)
    rstd = lax.rsqrt(var + EPS)
    return cen * rstd, rstd


def keep_mask(top, held, img, shape):
    row = lax.broadcasted_iota(jnp.int32, shape, 0)
    lo = top[img] * 16
    return jnp.logical_and(row >= lo, row < lo + held[img] * 16)


LN2 = math.log(2.0)
STAT = ((48, 49, 50, 51), (0, 1, 2, 3), (16, 17, 18, 19), (64, 65, 66, 67), (4, 5, 6, 7), (32, 33, 34, 35), (80, 81, 82, 83), (8, 9, 10, 11))


def head_tools(h, lane):
    a, b = 48 * h, 48 * h + 48
    t0, t1 = a // 128, (b - 1) // 128
    spans = [(t0, a - 128 * t0, min(b - 128 * t0, 128))]
    if t1 != t0:
        spans.append((t1, 0, b - 128 * t1))
    masks = [(t, jnp.logical_and(lane >= lo, lane < hi)) for t, lo, hi in spans]
    inside = functools.reduce(jnp.logical_or, [m for _, m in masks])

    def window(tiles):
        if len(spans) == 1:
            return tiles[t0]
        return jnp.where(masks[0][1], tiles[t0], tiles[t1])

    return masks, inside, window


def some_lanes(lane, which):
    return functools.reduce(jnp.logical_or, [lane == i for i in which])


def parted(lane, v):
    hi = v.astype(BF16)
    rest = v - hi.astype(F32)
    mid = rest.astype(BF16)
    lo = (rest - mid.astype(F32)).astype(BF16)
    first, second = (some_lanes(lane, [s[i] for s in STAT]) for i in (0, 1))
    return jnp.where(first, hi, jnp.where(second, mid, lo))


def attn_tiles(ref, rows, base, count=3):
    return [ref[rows, base + 128 * j : base + 128 * j + 128] for j in range(count)]


def attn_forward(img, half, r):
    rows = ds(img, 256)
    q, k, v = (attn_tiles(r.qkv, rows, 1152 * half + 384 * p) for p in range(3))
    lane = lax.broadcasted_iota(jnp.int32, (256, 128), 1)
    bias = jnp.where(keep_mask(r.top, r.held, img, (256, 128)), 0.0, NEG).astype(BF16)
    zero, one = jnp.zeros((256, 128), BF16), jnp.ones((256, 128), BF16)
    out, den = ([jnp.zeros((256, 128), F32) for _ in range(3)] for _ in range(2))
    top, tot = jnp.zeros((256, 128), F32), jnp.ones((256, 128), F32)
    for h in range(8):
        masks, inside, window = head_tools(h, lane)
        mask_lane = lane == STAT[h][3]
        qi = jnp.where(inside, window(q), jnp.where(mask_lane, one, zero))
        s = dot(qi, jnp.where(mask_lane, bias, window(k)), NT)
        m = jnp.max(s, axis=1, keepdims=True)
        e = jnp.exp2(s - m).astype(BF16)
        res = dot(e, jnp.concatenate([window(v), one], axis=1), NN)
        for j, mask in masks:
            out[j] = jnp.where(mask, res[:, :128], out[j])
            den[j] = jnp.where(mask, res[:, 128:], den[j])
        mine = some_lanes(lane, STAT[h][:3])
        top, tot = jnp.where(mine, m, top), jnp.where(mine, res[:, 128:], tot)
    ext = jnp.where(some_lanes(lane, [s[3] for s in STAT]), one, parted(lane, -(top + jnp.log2(tot))))
    r.ext[rows, 128 * half : 128 * half + 128] = ext
    for j in range(3):
        r.ho[rows, 384 * half + 128 * j : 384 * half + 128 * j + 128] = (out[j] / den[j]).astype(BF16)


def attn_backward(img, half, r):
    rows = ds(img, 256)
    q, k, v = (attn_tiles(r.qkv, rows, 1152 * half + 384 * p) for p in range(3))
    o, do = (attn_tiles(ref, rows, 384 * half) for ref in (r.ho, r.gheads))
    ext = r.ext[rows, 128 * half : 128 * half + 128]
    lane = lax.broadcasted_iota(jnp.int32, (256, 128), 1)
    bias = jnp.where(keep_mask(r.top, r.held, img, (256, 128)), 0.0, NEG).astype(BF16)
    zero, one = jnp.zeros((256, 128), BF16), jnp.ones((256, 128), BF16)
    feature = lax.broadcasted_iota(jnp.int32, (128, 128), 0)
    spot = lax.broadcasted_iota(jnp.int32, (128, 128), 1)
    inner = jnp.zeros((256, 128), F32)
    for j in range(3):
        prod = do[j].astype(F32) * o[j].astype(F32)
        hi = prod.astype(BF16)
        lo = (prod - hi.astype(F32)).astype(BF16)
        pick = jnp.zeros((128, 128), jnp.bool_)
        for h in range(8):
            first, last = max(48 * h - 128 * j, 0), min(48 * h + 48 - 128 * j, 128)
            if first < last:
                owned = jnp.logical_and(feature >= first, feature < last)
                pick = jnp.logical_or(pick, jnp.logical_and(owned, some_lanes(spot, STAT[h][:3])))
        pick = jnp.where(pick, -1.0, 0.0).astype(BF16)
        inner += dot(hi, pick, NN) + dot(lo, pick, NN)
    inner = parted(lane, inner)
    dq, dk, dv = ([zero] * 3 for _ in range(3))
    for h in range(8):
        masks, inside, window = head_tools(h, lane)
        mine = some_lanes(lane, STAT[h][:3])
        kw, dow = window(k), window(do)
        ones = jnp.where(mine, one, zero)
        ki = jnp.where(inside, kw, jnp.where(lane == STAT[h][3], bias, ones))
        qi = jnp.where(inside, window(q), ext)
        pt = jnp.exp2(dot(ki, qi, NT))
        dpt = dot(jnp.where(inside, window(v), ones), jnp.where(inside, dow, inner), NT)
        dst = (pt * dpt).astype(BF16)
        rv = dot(pt.astype(BF16), dow, NN).astype(BF16)
        rk = (dot(dst, qi, NN) * LN2).astype(BF16)
        rq = (dot(dst, kw, TN) * r.factor).astype(BF16)
        for j, mask in masks:
            dq[j] = jnp.where(mask, rq, dq[j])
            dk[j] = jnp.where(mask, rk, dk[j])
            dv[j] = jnp.where(mask, rv, dv[j])
    for p, parts in enumerate((dq, dk, dv)):
        for j in range(3):
            c = 1152 * half + 384 * p + 128 * j
            r.qkv[rows, c : c + 128] = parts[j]


def colsum(v):
    return jnp.sum(v, axis=0, keepdims=True)


def row(ref, i):
    return ref[i : i + 1, :]


def add_row(ref, i, v):
    ref[i : i + 1, :] += v


def stage_mask(r):
    def body(i):
        g = jnp.where(keep_mask(r.top, r.held, i, (256, 768)), r.tok[ds(i, 256), :].astype(F32), 0.0)
        add_row(r.acc, D_BIAS, colsum(g))
        r.tok[ds(i, 256), :] = g.astype(BF16)

    loop(4, body)


def stage_norm1(r):
    def body(i):
        xh, _ = normed(r.xin[ds(i, 256), :].astype(F32))
        r.low1[ds(i, 256), :] = (xh * row(r.par, A_GAIN) + row(r.par, A_SHIFT)).astype(BF16)

    loop(4, body)


def stage_qkv(half, r):
    cols = slice(1152 * half, 1152 * half + 1152)
    mine = slice(384 * half, 384 * half + 384)

    def body(i):
        w = r.wqkv[:, :, :, :, cols].reshape(768, 1152)
        p = dot(r.low1[ds(i, 256), :], w, NN)
        q = (p[:, :384] + r.par[H_BIAS : H_BIAS + 1, mine]) * (r.factor / LN2)
        v = p[:, 768:] + r.par[H_BIAS + 1 : H_BIAS + 2, mine]
        r.qkv[ds(i, 256), cols] = jnp.concatenate([q, p[:, 384:768], v], axis=1).astype(BF16)

    loop(4, body)


def stage_proj(r):
    def body(i):
        rows = ds(i, 256)
        w = r.wp[...].reshape(768, 768)
        x = r.xin[rows, :].astype(F32) + (dot(r.ho[rows, :], w, NN) + row(r.par, P_BIAS))
        r.resid[rows, :] = x
        xh, _ = normed(x)
        r.low2[rows, :] = (xh * row(r.par, M_GAIN) + row(r.par, M_SHIFT)).astype(BF16)

    loop(4, body)


def stage_up(n, r):
    cols = slice(768 * n, 768 * n + 768)

    def body(i):
        rows = ds(i, 256)
        z = dot(r.low2[rows, :], r.wu[:, :, :, :, cols].reshape(768, 768), NN) + row(r.par, U_BIAS + n)
        z2 = z * z
        t = jnp.tanh(z * (SQ + (SQ * CUBIC) * z2))
        hz = 0.5 * z
        r.act[rows, cols] = (hz + hz * t).astype(BF16)
        r.gp[rows, cols] = (0.5 + 0.5 * t + hz * (1.0 - t * t) * (SQ + (3 * SQ * CUBIC) * z2)).astype(BF16)

    loop(4, body)


def stage_down(r, first=0, count=4):
    def body(i):
        i = i + first
        rows = ds(i, 256)
        w = r.wd[...].reshape(3072, 768)
        x = r.resid[rows, :] + (dot(r.act[rows, :], w, NN) + row(r.par, D_BIAS))
        r.stage2[rows, :] = jnp.where(keep_mask(r.top, r.held, i, (256, 768)), x, 0.0).astype(BF16)

    loop(count, body)


def stage_dwd(n, r):
    cols = slice(256 * n, 256 * n + 256)

    def body(i):
        v = dot(r.act[:, ds(i, 768)], r.tok[:, cols], TN).astype(BF16)
        r.dwd[i // 2, i % 2, :, :, cols] = v.reshape(2, 384, 256)

    loop(4, body)


def stage_gact(n, r):
    cols = slice(768 * n, 768 * n + 768)
    y, x = n // 2, n % 2

    def body(i):
        rows = ds(i, 256)
        ga = dot(r.tok[rows, :], r.wd[y, x].reshape(768, 768), NT)
        gh = (ga * r.gp[rows, cols].astype(F32)).astype(BF16)
        add_row(r.acc, U_BIAS + n, colsum(gh.astype(F32)))
        r.gp[rows, cols] = gh

    loop(4, body)


def stage_dwu(n, r):
    cols = slice(768 * n, 768 * n + 768)

    def body(i):
        v = dot(r.low2[:, ds(i, 384)], r.gp[:, cols], TN).astype(BF16)
        r.dwu[i, :, :, n] = v.reshape(2, 2, 96, 768)

    loop(2, body)


def norm_back(grad, x, gain, acc, gain_row):
    xh, rstd = normed(x)
    add_row(acc, gain_row, colsum(grad * xh))
    add_row(acc, gain_row + 1, colsum(grad))
    u = grad * gain
    return (u - jnp.mean(u, axis=1, keepdims=True) - xh * jnp.mean(u * xh, axis=1, keepdims=True)) * rstd


def stage_gtwo(r, first=0, count=4):
    def body(i):
        rows = ds(i + first, 256)
        gt = dot(r.gp[rows, :], r.wu[...].reshape(768, 3072), NT)
        g = r.tok[rows, :].astype(F32) + norm_back(gt, r.resid[rows, :], row(r.par, M_GAIN), r.acc, M_GAIN)
        b = g.astype(BF16)
        add_row(r.acc, P_BIAS, colsum(b.astype(F32)))
        r.low2[rows, :] = b
        r.gp[rows, 0:768] = (g - b.astype(F32)).astype(BF16)

    loop(count, body)


def stage_dwp(r):
    def body(i):
        v = dot(r.ho[:, ds(i, 384)], r.low2[...], TN).astype(BF16)
        r.wu[i, :, :, :, 0:768] = v.reshape(2, 2, 96, 768)

    loop(2, body)


def stage_gheads(r):
    def body(i):
        r.gheads[ds(i, 256), :] = dot(r.low2[ds(i, 256), :], r.wp[...].reshape(768, 768), NT).astype(BF16)

    loop(4, body)


def stage_hbias(half, r):
    mine = slice(384 * half, 384 * half + 384)

    def body(i):
        d = r.qkv[ds(i, 256), 1152 * half : 1152 * half + 1152].astype(F32)
        r.acc[H_BIAS : H_BIAS + 1, mine] += colsum(d[:, :384])
        r.acc[H_BIAS + 1 : H_BIAS + 2, mine] += colsum(d[:, 768:])

    loop(4, body)


def stage_dwqkv(half, r):
    cols = slice(1152 * half, 1152 * half + 1152)
    into = slice(768 + 1152 * half, 1920 + 1152 * half)

    def body(i):
        v = dot(r.low1[:, ds(i, 384)], r.qkv[:, cols], TN).astype(BF16)
        r.wu[i, :, :, :, into] = v.reshape(2, 2, 96, 1152)

    loop(2, body)


def stage_gone(r, first=0, count=4):
    def body(i):
        rows = ds(i + first, 256)
        go = dot(r.qkv[rows, :], r.wqkv[...].reshape(768, 2304), NT)
        back = norm_back(go, r.xin[rows, :].astype(F32), row(r.par, A_GAIN), r.acc, A_GAIN)
        kept = r.low2[rows, :].astype(F32) + r.gp[rows, 0:768].astype(F32)
        r.stage[rows, :] = (kept + back).astype(BF16)

    loop(count, body)


def pieces(s):
    out = [(i, 96, i, 96 * s) for i in range(6)]
    out.append((6, 192, H_BIAS + s // 4, 192 * (s % 4)))
    out.append((7, 384, U_BIAS + s // 2, 384 * (s % 2)))
    return out


def spread_small(src, par):
    for s in range(8):
        for i, n, t, c in pieces(s):
            par[t : t + 1, c : c + n] = src[s // 4, s // 2 % 2, s % 2, i : i + 1, 0:n]


def gather_small(acc, dst):
    for s in range(8):
        dst[s // 4, s // 2 % 2, s % 2] = jnp.zeros((8, 384), F32)
        for i, n, t, c in pieces(s):
            dst[s // 4, s // 2 % 2, s % 2, i : i + 1, 0:n] = acc[t : t + 1, c : c + n]


class Links:
    def __init__(self, send, recv):
        z, f = lax.axis_index("dp"), lax.axis_index("fsdp")
        self.y, self.x, self.c = lax.div(f, 4), lax.rem(lax.div(f, 2), 2), lax.rem(f, 2)
        y, x, c = self.y, self.x, self.c
        self.z = z
        self.e = lax.rem(lax.div(z + 1, 2), 2)
        e = self.e

        def at(yy, xx, cc):
            return (z, 4 * yy + 2 * xx + cc)

        self.nx, self.ny, self.nd, self.nc = at(y, 1 - x, c), at(1 - y, x, c), at(1 - y, 1 - x, c), at(y, x, 1 - c)
        self.nz, self.nm, self.nw = (z + 1 - 2 * lax.rem(z, 2), f), (3 - z, f), (lax.rem(z + 2, 4), f)
        self.p1 = (y + e * (1 - 2 * y), x + (1 - e) * (1 - 2 * x))
        self.p2 = (y + (1 - e) * (1 - 2 * y), x + e * (1 - 2 * x))
        self.d1, self.d2 = at(*self.p1, c), at(*self.p2, c)
        self.send, self.recv, self.count = send, recv, 0
        self.started = []

    def greet(self):
        barrier = pltpu.get_barrier_semaphore()
        partners = (self.nx, self.ny, self.nd, self.nc, self.nz, self.nm, self.nw)
        for p in partners:
            pl.semaphore_signal(barrier, inc=1, device_id=p, device_id_type=MESH)
        pl.semaphore_wait(barrier, len(partners))

    def copy(self, src, dst, to):
        i = self.count
        self.count += 1
        c = pltpu.make_async_remote_copy(
            src_ref=src, dst_ref=dst, send_sem=self.send.at[i], recv_sem=self.recv.at[i], device_id=to, device_id_type=MESH
        )
        c.start()
        self.started.append(c)
        return c

    def sent(self, c):
        c.wait_send()
        self.started = [other for other in self.started if other is not c]

    def flush(self):
        for c in self.started:
            c.wait_send()
        self.started = []


def half_rows(rows, h):
    n = rows // 2
    return pl.ds(pl.multiple_of(h * n, n), n)


class Direct:
    def __init__(self, links, view, rows):
        l = self.l = links
        self.every = view(slice(0, 2), slice(0, 2), l.c, slice(0, rows))
        mine = view(l.y, l.x, l.c, slice(0, rows))
        self.hops = [l.copy(mine, mine, to) for to in (l.nx, l.ny, l.nd)]

    def share(self):
        for cp in self.hops:
            cp.wait_recv()
        self.core = self.l.copy(self.every, self.every, self.l.nc)

    def finish(self):
        self.core.wait_recv()


class Relay:
    def __init__(self, links, view, rows):
        l = self.l = links
        self.view, self.rows = view, rows
        mine = view(l.y, l.x, l.c, slice(0, rows))
        self.hops = [l.copy(mine, mine, to) for to in (l.nx, l.ny)]

    def turn(self):
        l, view, n = self.l, self.view, self.rows // 2
        for cp in self.hops:
            cp.wait_recv()
        one = view(l.y, 1 - l.x, l.c, slice(0, n))
        two = view(1 - l.y, l.x, l.c, slice(n, 2 * n))
        self.hops = [l.copy(one, one, l.ny), l.copy(two, two, l.nx)]

    def share(self):
        l = self.l
        for cp in self.hops:
            cp.wait_recv()
        every = self.view(slice(0, 2), slice(0, 2), l.c, slice(0, self.rows))
        self.core = l.copy(every, every, l.nc)

    def finish(self):
        self.core.wait_recv()


class Gather:
    def __init__(self, links, chunks):
        self.l, self.chunks, self.done, self.state = links, chunks, 0, [dict() for _ in chunks]

    def first(self, i):
        if i >= len(self.chunks):
            return
        l, (view, rows), st = self.l, self.chunks[i], self.state[i]
        full = view(l.y, l.x, l.c, slice(0, rows))
        st["p"] = l.copy(full, full, l.d1)
        part = view(l.y, l.x, l.c, slice(0, rows // 2))
        st["q"] = l.copy(part, part, l.d2)

    def at(self, i):
        if 0 <= i < len(self.chunks):
            return [(self.state[i], *self.chunks[i])]
        return []

    def tick(self):
        l, i = self.l, self.done
        self.done += 1
        for st, view, rows in self.at(i - 5):
            st["c"].wait_recv()
        for st, view, rows in self.at(i - 4):
            st["zp"].wait_recv()
            st["zd"].wait_recv()
            every = view(slice(0, 2), slice(0, 2), l.c, slice(0, rows))
            st["c"] = l.copy(every, every, l.nc)
        for st, view, rows in self.at(i - 2):
            st["q"].wait_recv()
            st["d"].wait_recv()
            part = view(1 - l.y, 1 - l.x, l.c, half_rows(rows, l.e))
            st["zd"] = l.copy(part, part, l.nz)
        for st, view, rows in self.at(i):
            st["p"].wait_recv()
            part = view(*l.p1, l.c, half_rows(rows, l.e))
            st["d"] = l.copy(part, part, l.d2)
            part = view(*l.p1, l.c, half_rows(rows, 1))
            st["zp"] = l.copy(part, part, l.nz)
        self.first(i + 2)

    def need(self, i):
        while self.done < i + 6:
            self.tick()

    def more(self):
        if self.done < len(self.chunks) + 5:
            self.tick()


class Reduce:
    def __init__(self, links):
        self.l, self.flying = links, []

    def push(self, view, rows, bufs, finish, advance=True):
        if advance:
            self.advance()
        st = dict(view=view, rows=rows, bufs=bufs, finish=finish, step=0)
        l = self.l
        st["c"] = l.copy(view(slice(0, 2), slice(0, 2), 1 - l.c, slice(0, rows)), bufs["c"](), l.nc)
        self.flying.append(st)

    def advance(self):
        for st in list(self.flying):
            st["step"] += 1
            getattr(self, "step%d" % st["step"])(st)

    def step1(self, st):
        l, view, b, n = self.l, st["view"], st["bufs"], st["rows"]
        st["c"].wait_recv()
        got = b["c"]()
        for y in range(2):
            for x in range(2):
                mine = view(y, x, l.c, slice(0, n))
                mine[...] += got[y, x]
        h0, h1 = slice(0, n // 2), slice(n // 2, n)
        st["x"] = l.copy(view(slice(0, 2), 1 - l.x, l.c, h0), b["x"](0), l.nx)
        st["y"] = l.copy(view(1 - l.y, slice(0, 2), l.c, h1), b["x"](1), l.ny)

    def step2(self, st):
        l, view, b, n = self.l, st["view"], st["bufs"], st["rows"]
        h0, h1 = slice(0, n // 2), slice(n // 2, n)
        st["x"].wait_recv()
        st["y"].wait_recv()
        for i in range(2):
            mine = view(i, l.x, l.c, h0)
            mine[...] += b["x"](0)[i]
            mine = view(l.y, i, l.c, h1)
            mine[...] += b["x"](1)[i]
        st["x"] = l.copy(view(1 - l.y, l.x, l.c, h0), b["y"](0), l.ny)
        st["y"] = l.copy(view(l.y, 1 - l.x, l.c, h1), b["y"](1), l.nx)

    def step3(self, st):
        l, view, b, n = self.l, st["view"], st["bufs"], st["rows"]
        st["x"].wait_recv()
        st["y"].wait_recv()
        mine = view(l.y, l.x, l.c, slice(0, n // 2))
        mine[...] += b["y"](0)[...]
        mine = view(l.y, l.x, l.c, slice(n // 2, n))
        mine[...] += b["y"](1)[...]
        st["z"] = l.copy(view(l.y, l.x, l.c, half_rows(n, 1 - l.e)), b["z"](0), l.nz)

    def step4(self, st):
        l, view, b, n = self.l, st["view"], st["bufs"], st["rows"]
        st["z"].wait_recv()
        l.sent(st["z"])
        mine = view(l.y, l.x, l.c, half_rows(n, l.e))
        mine[...] += b["z"](0)[...]
        st["z"] = l.copy(mine, b["z"](1), l.nm)

    def step5(self, st):
        l, view, b, n = self.l, st["view"], st["bufs"], st["rows"]
        st["z"].wait_recv()
        l.sent(st["z"])
        mine = view(l.y, l.x, l.c, half_rows(n, l.e))
        mine[...] += b["z"](1)[...]
        st["z"] = l.copy(mine, b["z"](2), l.nz)

    def step6(self, st):
        l = self.l
        st["z"].wait_recv()
        st["view"](l.y, l.x, l.c, half_rows(st["rows"], 1 - l.e))[...] = st["bufs"]["z"](2)[...]
        st["finish"](st["view"](l.y, l.x, l.c, slice(0, st["rows"])))
        self.flying = [other for other in self.flying if other is not st]


class ReduceSmall:
    def __init__(self, links, r):
        l = self.l = links
        self.r = r
        self.hops = [l.copy(r.smallg.at[:, :, 1 - l.c], r.cs, l.nc)]

    def wait(self):
        for cp in self.hops:
            cp.wait_recv()

    def plane(self):
        l, r = self.l, self.r
        self.wait()
        for y in range(2):
            for x in range(2):
                r.smallg[y, x, l.c] += r.cs[y, x]
        to = ((l.y, 1 - l.x, l.nx), (1 - l.y, l.x, l.ny), (1 - l.y, 1 - l.x, l.nd))
        self.hops = [l.copy(r.smallg.at[y, x, l.c], r.xs.at[i], p) for i, (y, x, p) in enumerate(to)]

    def replicas(self):
        l, r = self.l, self.r
        self.wait()
        r.zs[l.z] = r.smallg[l.y, l.x, l.c] + r.xs[0] + r.xs[1] + r.xs[2]
        self.hops = [l.copy(r.zs.at[l.z], r.zs.at[l.z], p) for p in (l.nz, l.nm, l.nw)]

    def total(self):
        r = self.r
        self.wait()
        r.fs[...] = (r.zs[0] + r.zs[1]) + (r.zs[2] + r.zs[3])


class Refs:
    pass


NAMES = (
    "top", "held", "tok_h", "cot_h", "v0", "v1", "v2", "v3", "v4", "v5", "v6", "v7", "wqkv_h", "wp_h", "wu_h", "wd_h",
    "out_h", "tg_h", "fq_h", "fp_h", "fu_h", "fd_h", "fs",
    "tok", "low1", "qkv", "ext", "ho", "resid", "low2", "act", "gp", "wqkv", "wp", "wu", "wd", "dwd", "dwu",
    "small", "par", "acc", "smallg", "cd", "xd", "yd", "zd", "cq", "xq", "yq", "zq", "cs", "xs", "zs",
    "local", "send", "recv",
)


def set_views(r):
    r.factor = 1.0 / math.sqrt(768 // HEADS)
    r.xin = r.tok
    r.stage, r.gheads, r.stage2 = (r.gp.at[:, 768 * i : 768 * i + 768] for i in (1, 2, 3))


def fused_kernel(*args):
    r = Refs()
    for name, ref in zip(NAMES, args, strict=True):
        setattr(r, name, ref)
    set_views(r)
    l = Links(r.send, r.recv)
    y, x, c = l.y, l.x, l.c
    locals_ = []

    def local(src, dst):
        i = len(locals_)
        cp = pltpu.make_async_copy(src, dst, r.local.at[i])
        cp.start()
        locals_.append(cp)
        return cp

    def qcols(half, part):
        a, b = 768 * part + 384 * half, 1152 * half + 384 * part
        return slice(a, a + 384), slice(b, b + 384)

    for i, v in enumerate((r.v0, r.v1, r.v2, r.v3, r.v4, r.v5, r.v6, r.v7)):
        n = v.shape[0]
        r.small[y, x, c, i : i + 1, 0:n] = v[...].astype(F32).reshape(1, n)
    load_q = [
        [local(r.wqkv_h.at[:, a], r.wqkv.at[y, x, c, :, b]) for a, b in (qcols(half, part) for part in range(3))]
        for half in range(2)
    ]
    load_tok = local(r.tok_h, r.tok)
    load_w = [local(r.wp_h, r.wp.at[y, x, c]), local(r.wu_h, r.wu.at[y, x, c]), local(r.wd_h, r.wd.at[y, x, c])]
    l.greet()

    def qview(half):
        k = slice(1152 * half, 1152 * half + 1152)
        return lambda a, b, d, s: r.wqkv.at[a, b, d, s, k]

    def uview(n):
        k = slice(768 * n, 768 * n + 768)
        return lambda a, b, d, s: r.wu.at[a, b, d, s, k]

    chunks = [(lambda a, b, d, s: r.wp.at[a, b, d, s, :], 96)]
    chunks += [(uview(n), 96) for n in range(4)]
    chunks += [(functools.partial(lambda k, a, b, d, s: r.wd.at[a, b, d, k, s, :], n), 96) for n in range(4)]
    g_small = Direct(l, lambda a, b, d, s: r.small.at[a, b, d, s, :], 8)
    for cp in load_q[0]:
        cp.wait()
    g_first = Direct(l, qview(0), 96)
    for cp in load_q[1] + load_w + [load_tok]:
        cp.wait()
    g_second = Relay(l, qview(1), 96)
    g = Gather(l, chunks)
    r.acc[...] = jnp.zeros_like(r.acc)
    g_small.share()
    g_first.share()
    g.first(0)
    g_small.finish()
    spread_small(r.small, r.par)
    stage_norm1(r)
    g_first.finish()

    stage_qkv(0, r)
    g_second.turn()
    g.first(1)
    loop(4, lambda i: attn_forward(i, 0, r))
    g_second.share()
    g.more()
    g_second.finish()
    stage_qkv(1, r)
    g.more()
    loop(2, lambda i: attn_forward(i, 1, r))
    g.more()
    loop(2, lambda i: attn_forward(i + 2, 1, r))
    g.more()
    g.more()
    g.need(0)
    stage_proj(r)
    load_cot = local(r.cot_h, r.tok)
    for n in range(4):
        g.need(1 + n)
        stage_up(n, r)
    g.more()

    red = Reduce(l)

    def fam_d(s):
        return dict(c=lambda: r.cd.at[s], x=lambda t: r.xd.at[s, t], y=lambda t: r.yd.at[s, t], z=lambda t: r.zd.at[s, t])

    def fam_q(s, k):
        return dict(
            c=lambda: r.cq.at[s, :, :, :, k], x=lambda t: r.xq.at[s, t, :, :, k],
            y=lambda t: r.yq.at[s, t, :, k], z=lambda t: r.zq.at[s, t, :, k],
        )

    finals = []

    def to(ref):
        return lambda mine: finals.append(local(mine, ref))

    def push_d(n):
        k = slice(256 * n, 256 * n + 256)
        red.push(lambda a, b, d, s: r.dwd.at[a, b, d, s, k], 384, fam_d(n % 2), to(r.fd_h.at[:, k]))

    def push_u(n):
        k = slice(768 * n, 768 * n + 768)
        red.push(lambda a, b, d, s: r.dwu.at[a, b, d, n, s, :], 96, fam_q(n % 2, slice(0, 768)), to(r.fu_h.at[:, k]))

    def push_p():
        red.push(lambda a, b, d, s: r.wu.at[a, b, d, s, 0:768], 96, fam_q(0, slice(0, 768)), to(r.fp_h))

    def push_q(half, part, advance):
        a, b = qcols(half, part)
        k = slice(768 + b.start, 768 + b.stop)
        bufs = fam_q(1 - half, slice(384 * part, 384 * part + 384))
        red.push(lambda i, j, d, s: r.wu.at[i, j, d, s, k], 96, bufs, to(r.fq_h.at[:, a]), advance)

    load_cot.wait()
    stage_mask(r)
    stage_dwd(0, r)
    g.more()
    push_d(0)
    stage_dwd(1, r)
    g.more()
    push_d(1)
    stage_dwd(2, r)
    g.need(8)
    stage_gact(0, r)
    stage_gact(1, r)
    push_d(2)
    stage_gact(2, r)
    stage_gact(3, r)
    l.flush()
    stage_dwu(0, r)
    stage_dwu(1, r)
    push_u(0)
    stage_dwu(2, r)
    stage_dwu(3, r)
    stage_gtwo(r, 0, 2)
    push_u(1)
    stage_gtwo(r, 2, 2)
    load_tok = local(r.tok_h, r.tok)
    stage_dwp(r)
    push_u(2)
    stage_gheads(r)
    loop(1, lambda i: attn_backward(i, 0, r))
    push_u(3)
    loop(2, lambda i: attn_backward(i + 1, 0, r))
    push_p()
    loop(1, lambda i: attn_backward(i + 3, 0, r))
    stage_dwqkv(0, r)
    for part in range(3):
        push_q(0, part, part == 0)
    stage_hbias(0, r)
    loop(2, lambda i: attn_backward(i, 1, r))
    red.advance()
    loop(2, lambda i: attn_backward(i + 2, 1, r))
    stage_dwqkv(1, r)
    for part in range(3):
        push_q(1, part, part == 0)
    stage_hbias(1, r)
    load_tok.wait()
    stage_gone(r, 0, 2)
    red.advance()
    stage_gone(r, 2, 2)
    store_tg = local(r.stage, r.tg_h)
    gather_small(r.acc, r.smallg)
    rs = ReduceSmall(l, r)
    stage_down(r, 0, 2)
    rs.plane()
    red.advance()
    stage_down(r, 2, 2)
    store_out = local(r.stage2, r.out_h)
    rs.replicas()
    red.advance()
    rs.total()
    while red.flying:
        red.advance()
    l.flush()
    store_tg.wait()
    store_out.wait()
    for cp in finals:
        cp.wait()


def fused_call(top, held, tokens, cotangent, vectors, wqkv, wp, wu, wd):
    rows = tokens.shape[0]
    sds = jax.ShapeDtypeStruct
    v = pltpu.VMEM
    hbm = pl.BlockSpec(memory_space=pl.ANY)
    dma = pltpu.SemaphoreType.DMA
    b = lambda *s: v(s, BF16)
    f = lambda *s: v(s, F32)
    return pl.pallas_call(
        fused_kernel,
        out_shape=(
            sds((rows, 768), BF16), sds((rows, 768), BF16), sds((96, 2304), BF16), sds((96, 768), BF16),
            sds((96, 3072), BF16), sds((384, 768), BF16), sds((8, 384), F32),
        ),
        in_specs=[pl.BlockSpec(memory_space=pltpu.SMEM)] * 2 + [hbm] * 2 + [pl.BlockSpec(memory_space=v)] * 8 + [hbm] * 4,
        out_specs=[hbm] * 6 + [pl.BlockSpec(memory_space=v)],
        scratch_shapes=[
            b(rows, 768), b(rows, 768), b(rows, 2304), b(rows, 256), b(rows, 768), f(rows, 768), b(rows, 768),
            b(rows, 3072), b(rows, 3072),
            b(2, 2, 2, 96, 2304), b(2, 2, 2, 96, 768), b(2, 2, 2, 96, 3072), b(2, 2, 2, 4, 96, 768), b(2, 2, 2, 384, 768),
            b(2, 2, 2, 4, 96, 768),
            f(2, 2, 2, 8, 384), f(16, 768), f(16, 768), f(2, 2, 2, 8, 384),
            b(2, 2, 2, 384, 256), b(2, 2, 2, 192, 256), b(2, 2, 192, 256), b(2, 3, 192, 256),
            b(2, 2, 2, 96, 1152), b(2, 2, 2, 48, 1152), b(2, 2, 48, 1152), b(2, 3, 48, 1152),
            f(2, 2, 8, 384), f(3, 8, 384), f(4, 8, 384),
            dma((40,)), dma((200,)), dma((200,)),
        ],
        compiler_params=pltpu.CompilerParams(collective_id=0, has_side_effects=True, vmem_limit_bytes=64 * 2**20),
        cost_estimate=pl.CostEstimate(flops=46 * 10**9, bytes_accessed=20 * 10**6, transcendentals=12 * 10**6),
    )(top, held, tokens, cotangent, *vectors, wqkv, wp, wu, wd)


def finish_kernel(out, tg, fq, fp, fu, fd, fs, *rest):
    outs, (bq, bp, bu, bd, wq, wp, wu, wd, bo, bt, sems) = rest[:14], rest[14:]
    out_o, tg_o, s0, s1, q_o, s6, p_o, s2, s3, s4, u_o, s7, d_o, s5 = outs
    whole = []
    for i, (src, b, dst) in enumerate(((out, bo, out_o), (tg, bt, tg_o))):
        for h in range(2):
            k = slice(512 * h, 512 * h + 512)
            args = (src.at[k], b.at[k], sems.at[10 + 2 * i + h]), (b.at[k], dst.at[k], sems.at[14 + 2 * i + h])
            whole.append([pltpu.make_async_copy(*a) for a in args])
    mats = [(fd, bd, wd, d_o), (fu, bu, wu, u_o), (fq, bq, wq, q_o), (fp, bp, wp, p_o)]
    loads = [pltpu.make_async_copy(src, b, sems.at[2 + i]) for i, (src, b, _, _) in enumerate(mats)]
    for cp in [w[0] for w in whole] + loads:
        cp.start()
    for i, o in enumerate((s0, s1, s2, s3, s4, s5, s6, s7)):
        n = o.shape[0]
        o[...] = fs[i : i + 1, 0:n].reshape(n)
    for cp in whole:
        cp[0].wait()
        cp[1].start()
    stores = [cp[1] for cp in whole]
    for i, (_, b, w, o) in enumerate(mats):
        loads[i].wait()
        w[...] = b[...].astype(F32)
        stores.append(pltpu.make_async_copy(w, o, sems.at[6 + i]))
        stores[-1].start()
    for cp in stores:
        cp.wait()


def finish_call(*parts):
    sds = jax.ShapeDtypeStruct
    v = pltpu.VMEM
    hbm, vmem = pl.BlockSpec(memory_space=pl.ANY), pl.BlockSpec(memory_space=v)
    vec = lambda n: (sds((n,), F32), vmem)
    mat = lambda a: (sds(a.shape, F32), hbm)
    out, tg, fq, fp, fu, fd, fs = parts
    outs = (
        (sds(out.shape, BF16), hbm), (sds(tg.shape, BF16), hbm), vec(96), vec(96), mat(fq), vec(192), mat(fp), vec(96),
        vec(96), vec(96), mat(fu), vec(384), mat(fd), vec(96),
    )
    mats = (fq, fp, fu, fd)
    return pl.pallas_call(
        finish_kernel,
        out_shape=tuple(o[0] for o in outs),
        in_specs=[hbm] * 6 + [vmem],
        out_specs=[o[1] for o in outs],
        scratch_shapes=[v(a.shape, BF16) for a in mats] + [v(a.shape, F32) for a in mats] + [v(out.shape, BF16)] * 2 + [pltpu.SemaphoreType.DMA((18,))],
        compiler_params=pltpu.CompilerParams(vmem_limit_bytes=64 * 2**20),
    )(*parts)


PLAIN = (
    "top", "held", "tok_h", "cot_h", "par", "wqkv_h", "wp_h", "wu_h", "wd_h", "out_h", "tg_h", "gq_h", "gp_h", "gu_h",
    "gd_h", "acc", "xin", "tok", "low1", "qkv", "ext", "ho", "resid", "low2", "act", "gp", "wqkv", "wp", "wu", "wd",
    "dwd", "dwu", "local",
)


def plain_kernel(*args):
    r = Refs()
    for name, ref in zip(PLAIN, args, strict=True):
        setattr(r, name, ref)
    xin = r.xin
    set_views(r)
    r.xin = xin

    def every(pairs):
        copies = [pltpu.make_async_copy(src, dst, r.local.at[i]) for i, (src, dst) in enumerate(pairs)]
        for cp in copies:
            cp.start()
        for cp in copies:
            cp.wait()

    def mixed(ref, k):
        return ref.at[:, :, :, :, k]

    blocks = [(p, h, slice(768 * p + 384 * h, 768 * p + 384 * h + 384), 1152 * h + 384 * p) for h in range(2) for p in range(3)]
    every(
        [(r.tok_h, r.xin), (r.cot_h, r.tok), (r.wp_h, r.wp), (r.wu_h, r.wu), (r.wd_h, r.wd)]
        + [(mixed(r.wqkv_h, a), mixed(r.wqkv, slice(b, b + 384))) for _, _, a, b in blocks]
    )
    r.acc[...] = jnp.zeros_like(r.acc)
    stage_mask(r)
    stage_norm1(r)
    for half in range(2):
        stage_qkv(half, r)
        loop(4, lambda i: attn_forward(i, half, r))
    stage_proj(r)
    for n in range(4):
        stage_up(n, r)
    for n in range(3):
        stage_dwd(n, r)
    for n in range(4):
        stage_gact(n, r)
    for n in range(4):
        stage_dwu(n, r)
    stage_gtwo(r)
    stage_dwp(r)
    stage_gheads(r)
    for half in range(2):
        loop(4, lambda i: attn_backward(i, half, r))
        stage_dwqkv(half, r)
        stage_hbias(half, r)
    stage_gone(r)
    stage_down(r)
    every(
        [(r.stage, r.tg_h), (r.stage2, r.out_h), (r.dwd, r.gd_h), (mixed(r.wu, slice(0, 768)), r.gp_h)]
        + [(r.dwu.at[:, :, :, n], mixed(r.gu_h, slice(768 * n, 768 * n + 768))) for n in range(4)]
        + [(mixed(r.wu, slice(768 + b, 1152 + b)), mixed(r.gq_h, a)) for _, _, a, b in blocks]
    )


def plain_call(top, held, tokens, cotangent, par, wqkv, wp, wu, wd):
    rows = tokens.shape[0]
    sds = jax.ShapeDtypeStruct
    v = pltpu.VMEM
    hbm = pl.BlockSpec(memory_space=pl.ANY)
    b = lambda *s: v(s, BF16)
    f = lambda *s: v(s, F32)
    o = lambda *s: sds((2, 2, 2) + s, BF16)
    return pl.pallas_call(
        plain_kernel,
        out_shape=(
            sds((rows, 768), BF16), sds((rows, 768), BF16), o(96, 2304), o(96, 768), o(96, 3072), o(384, 768),
            sds((16, 768), F32),
        ),
        in_specs=[pl.BlockSpec(memory_space=pltpu.SMEM)] * 2 + [hbm] * 2 + [pl.BlockSpec(memory_space=v)] + [hbm] * 4,
        out_specs=[hbm] * 6 + [pl.BlockSpec(memory_space=v)],
        scratch_shapes=[
            b(rows, 768), b(rows, 768), b(rows, 768), b(rows, 2304), b(rows, 256), b(rows, 768), f(rows, 768), b(rows, 768),
            b(rows, 3072), b(rows, 3072),
            b(2, 2, 2, 96, 2304), b(2, 2, 2, 96, 768), b(2, 2, 2, 96, 3072), b(2, 2, 2, 4, 96, 768), b(2, 2, 2, 384, 768),
            b(2, 2, 2, 4, 96, 768), pltpu.SemaphoreType.DMA((16,)),
        ],
        compiler_params=pltpu.CompilerParams(vmem_limit_bytes=64 * 2**20),
        cost_estimate=pl.CostEstimate(flops=46 * 10**9, bytes_accessed=40 * 10**6, transcendentals=12 * 10**6),
    )(top, held, tokens, cotangent, par, wqkv, wp, wu, wd)


def pack_small(*vectors):
    n = max(v.shape[0] for v in vectors)
    return jnp.stack([jnp.pad(v.astype(F32), (0, n - v.shape[0])) for v in vectors])


def fused_shards(tokens, cotangent, crop_rows, crop_top, ag, ash, hw, hb, pw, pb, mg, ms, uw, ub, dw, db):
    vectors = (ag, ash, pb, mg, ms, db, hb, ub)
    parts = fused_call(crop_top, crop_rows, tokens, cotangent, vectors, hw, pw, uw, dw.reshape(4, 96, 768))
    return tuple(finish_call(*parts))


def plain_shards(tokens, cotangent, crop_rows, crop_top, ag, ash, hw, hb, pw, pb, mg, ms, uw, ub, dw, db):
    size = lax.axis_size("fsdp")

    def gather(a, shape):
        return lax.all_gather(a, "fsdp", axis=0, tiled=True).reshape((2, 2, 2) + shape)

    def reduce(a):
        part = a.reshape((-1, a.shape[-1]))
        part = lax.psum_scatter(part, "fsdp", scatter_dimension=0, tiled=True)
        return lax.psum(part, "dp")

    n = ag.shape[0]
    small = lax.all_gather(pack_small(ag, ash, pb, mg, ms, db, hb, ub), "fsdp", axis=0)
    six = small[:, :6, :n].transpose(1, 0, 2).reshape(6, -1)
    par = jnp.concatenate([six, small[:, 6, : 2 * n].reshape(2, -1), small[:, 7].reshape(4, -1), jnp.zeros((4, 768), F32)])
    out, tg, gq, gp, gu, gd, acc = plain_call(
        crop_top, crop_rows, tokens, cotangent, par, gather(hw, (96, 2304)), gather(pw, (96, 768)),
        gather(uw, (96, 3072)), gather(dw, (4, 96, 768)),
    )
    six = acc[:6].reshape(6, size, -1).transpose(1, 0, 2)
    pieces = jnp.concatenate([six, acc[6:8].reshape(size, 2, -1), acc[8:12].reshape(size, 4, -1)], axis=1)
    s = lax.psum(lax.psum_scatter(pieces, "fsdp", scatter_dimension=0, tiled=True), "dp")[0]
    gq, gp, gu, gd = (reduce(a).astype(F32) for a in (gq, gp, gu, gd))
    return (
        out, tg, s[0], s[1], gq, s[6:8].reshape(-1), gp, s[2],
        s[3], s[4], gu, s[8:12].reshape(-1), gd, s[5],
    )


def solution(mesh):
    rows = P(("dp", "fsdp"), None)
    vec, mat = P("fsdp"), P("fsdp", None)
    fits = mesh.shape["dp"] == 4 and mesh.shape["fsdp"] == 8
    return jax.shard_map(
        fused_shards if fits else plain_shards,
        mesh=mesh,
        in_specs=(rows, rows, P(("dp", "fsdp")), P(("dp", "fsdp")), vec, vec, mat, vec, mat, vec, vec, vec, mat, vec, mat, vec),
        out_specs=(rows, rows, vec, vec, mat, vec, mat, vec, vec, vec, mat, vec, mat, vec),
        check_vma=False,
    )
```
